32 devices in a mesh: ctx: 16 (over z, y, x), round: 2 (over core).
Axes of the slice: x: 2, y: 2, z: 4, core: 2. Of those that a mesh axis runs over, the one named last changes fastest.
Arguments:
- x2: bfloat16 [4096, 1024], P('ctx'), may hold values from -16 to 16
- out_grad: bfloat16 [4096, 1024], P('ctx'), may hold values from -6 to 6
- w_qk: bfloat16 [1024, 1024], replicated, may hold values from -0.3125 to 0.3125
- w_v: bfloat16 [1024, 1024], replicated, may hold values from -0.1875 to 0.1875
- sort_slot: int32 [2, 4096], P(None, 'ctx'), may hold values from 0 to 4095, as said below
- source_pos: int32 [2, 4096], P('round', 'ctx'), may hold values from 0 to 4095, as said below
Outputs:
- grad_x2: bfloat16 [4096, 1024], P(('ctx', 'round'))
- grad_w_qk: float32 [1024, 1024], P(('ctx', 'round'))
- grad_w_v: float32 [1024, 1024], P(('ctx', 'round'))
The draws below stay inside these ranges and needn't reach their ends.
Inputs may be any that keep to these rules, and one draw needn't show every extreme that they name: `sort_slot`: for each round a permutation of the positions. Of the 256 positions k * 256 to (k + 1) * 256 - 1, at most 32 have sorted positions in any one range j * 256 to (j + 1) * 256 - 1 in one round, and in every round some pair of ranges reaches 32. For each round the inverse permutation of sort_slot: sort_slot[r, source_pos[r, s]] = s.
All inputs are finite; a program needn't handle non-finite values.
Results may differ from the reference program's by a relative error of at most 0.013.
The reference program's roundings to bfloat16 on the way count: a program that leaves them out, or rounds other values in their place, can miss the bound.
Values may be sent and summed in bfloat16 or wider, within the bound.
No kernel may reach another device: no remote copies, remote signals or barrier semaphores. Data moves between devices by JAX's collectives and lax.ppermute only.
A program may use at most 128 MiB of HBM per device.

```python
import jax
import jax.numpy as jnp
from jax import lax

D = 1024
HEADS = 16
HEAD_DIM = 64
SPAN = 256
T_DEV = 256
SEQ = 4096


def sorted_orders(key):
    devices = SEQ // T_DEV
    base = T_DEV // devices
    slots_all = []
    sources_all = []
    for hround in range(2):
        round_key = jax.random.fold_in(key, 100 + hround)
        keys = jax.random.split(round_key, 5)
        pairing = jax.random.permutation(keys[0], devices).astype(jnp.int32)
        excess = jax.random.randint(keys[1], (devices // 2,), 0, base + 1).astype(jnp.int32)
        excess = excess.at[0].set(base)
        weights = jnp.zeros((devices,), jnp.int32)
        weights = weights.at[pairing[:devices // 2]].set(base + excess)
        weights = weights.at[pairing[devices // 2:]].set(base - excess)
        upper = jnp.cumsum(weights).astype(jnp.int32)
        targets = jax.random.permutation(keys[2], devices).astype(jnp.int32)
        orders = jax.vmap(lambda k: jax.random.permutation(k, T_DEV))(jax.random.split(keys[3], devices)).astype(jnp.int32)
        place = jnp.argsort(orders, axis=1).astype(jnp.int32)
        shifted = jnp.sum((upper[None, None, :] <= place[:, :, None]).astype(jnp.int32), axis=2)
        source_dev = jnp.arange(devices, dtype=jnp.int32)[:, None]
        dest = targets[(source_dev + shifted) % devices]
        shuffles = jax.vmap(lambda k: jax.random.permutation(k, T_DEV))(jax.random.split(keys[4], devices)).astype(jnp.int32)
        slot = shuffles[dest, place]
        sorted_pos = (dest * T_DEV + slot).reshape(-1).astype(jnp.int32)
        inverse = jnp.zeros((SEQ,), jnp.int32).at[sorted_pos].set(jnp.arange(SEQ, dtype=jnp.int32))
        slots_all.append(sorted_pos)
        sources_all.append(inverse)
    return (jnp.stack(slots_all), jnp.stack(sources_all))


def draw_sort_slot(key, part):
    slots, sources = sorted_orders(key)
    return slots


def draw_source_pos(key, part):
    slots, sources = sorted_orders(key)
    return sources


def draw_x2(key, part):
    key = jax.random.fold_in(key, 7)
    keys = jax.random.split(key, 2)
    blocks = SEQ // T_DEV
    width_block = D // (2 * blocks)
    partner = jax.random.permutation(keys[0], 2 * blocks)[:blocks]
    row_block = jnp.arange(SEQ) // T_DEV
    col_block = jnp.arange(D) // width_block
    boost = jnp.where(col_block[None, :] == partner[row_block][:, None], 3.0, 1.0)
    values = jnp.clip(jax.random.normal(keys[1], (SEQ, D), jnp.float32), -5.0, 5.0) * boost
    return values.astype(jnp.bfloat16)


def shard_levels(rng, dims, cuts, least, top_value):
    level, own = 1.0, jax.random.fold_in(rng, 6)
    for position, parts in cuts:
        heights = jnp.exp(jax.random.uniform(jax.random.fold_in(own, position), (parts,), jnp.float32, least / len(cuts), top_value / len(cuts)))
        level = level * jnp.repeat(heights, dims[position] // parts).reshape([-1 if axis == position else 1 for axis in range(len(dims))])
    return level


def normal_values(rng, shape, width, most, shards=(), kind=jnp.bfloat16):
    drawn = jax.random.normal(rng, shape, jnp.float32) * width
    if len(shards) > 0:
        drawn = shard_levels(rng, shape, shards, -0.22, 0.18) * drawn
    return jnp.clip(drawn, min=-most, max=most).astype(kind)


def setup_inputs(seed: int = 0) -> dict:
    key_list = jax.random.split(jax.random.key(seed), 7)
    x2 = draw_x2(jax.random.fold_in(key_list[6], 71), 0)
    out_grad = normal_values(key_list[1], (SEQ, D), 1.0, 6.0, ((0, 16),))
    w_qk = normal_values(key_list[2], (D, D), (1.6 * D ** -0.5), 0.3125)
    w_v = normal_values(key_list[3], (D, D), D ** -0.5, 0.1875)
    sort_slot = draw_sort_slot(jax.random.fold_in(key_list[6], 71), 0)
    source_pos = draw_source_pos(jax.random.fold_in(key_list[6], 71), 0)
    return {"x2": x2, "out_grad": out_grad, "w_qk": w_qk, "w_v": w_v, "sort_slot": sort_slot, "source_pos": source_pos}


masked_score = -1.0e9


def span_keys(rows):
    count = rows.shape[0] // SPAN
    blocks = rows.reshape(count, SPAN, rows.shape[1])
    return blocks, jnp.concatenate([jnp.roll(blocks, 1, axis=0), blocks], axis=1)


def scores_of(q_block, k_block):
    q_heads = q_block.reshape(SPAN, HEADS, HEAD_DIM).astype(jnp.float32)
    k_heads = k_block.reshape(2 * SPAN, HEADS, HEAD_DIM).astype(jnp.float32)
    scores = jnp.einsum("qhd,khd->hqk", q_heads, k_heads) * (HEAD_DIM ** -0.5)
    selfpos = jnp.arange(2 * SPAN)[None, :] == jnp.arange(SPAN)[:, None] + SPAN
    return jnp.where(selfpos[None], masked_score, scores)


def forward_span(items):
    q_block, k_block, v_block = items
    scores = scores_of(q_block, k_block)
    top = jnp.max(scores, axis=2, keepdims=True)
    lse = top + jnp.log(jnp.sum(jnp.exp(scores - top), axis=2, keepdims=True))
    probs = lax.optimization_barrier(jnp.exp(scores - lse).astype(jnp.bfloat16)).astype(jnp.float32)
    v_heads = v_block.reshape(2 * SPAN, HEADS, HEAD_DIM).astype(jnp.float32)
    output = jnp.einsum("hqk,khd->qhd", probs, v_heads).reshape(SPAN, D)
    return output, lse[:, :, 0].T


def backward_span(items):
    q_block, k_block, v_block, g_block, lse_block, delta_block = items
    scores = scores_of(q_block, k_block)
    weights = jnp.exp(scores - lse_block.T[:, :, None])
    g_heads = g_block.reshape(SPAN, HEADS, HEAD_DIM).astype(jnp.float32)
    v_heads = v_block.reshape(2 * SPAN, HEADS, HEAD_DIM).astype(jnp.float32)
    k_heads = k_block.reshape(2 * SPAN, HEADS, HEAD_DIM).astype(jnp.float32)
    q_heads = q_block.reshape(SPAN, HEADS, HEAD_DIM).astype(jnp.float32)
    rounded = lax.optimization_barrier(weights.astype(jnp.bfloat16)).astype(jnp.float32)
    grad_val = jnp.einsum("hqk,qhd->khd", rounded, g_heads)
    inner = jnp.einsum("qhd,khd->hqk", g_heads, v_heads)
    dscore = weights * (inner - delta_block.T[:, :, None])
    dscore = lax.optimization_barrier(dscore.astype(jnp.bfloat16)).astype(jnp.float32)
    grad_q = jnp.einsum("hqk,khd->qhd", dscore, k_heads) * (HEAD_DIM ** -0.5)
    grad_k = jnp.einsum("hqk,qhd->khd", dscore, q_heads) * (HEAD_DIM ** -0.5)
    return grad_q.reshape(SPAN, D), grad_k.reshape(2 * SPAN, D), grad_val.reshape(2 * SPAN, D)


def reference(x2, out_grad, w_qk, w_v, sort_slot, source_pos):
    count = SEQ // SPAN
    qk = jnp.dot(x2, w_qk, preferred_element_type=jnp.float32).astype(jnp.bfloat16)
    val = jnp.dot(x2, w_v, preferred_element_type=jnp.float32).astype(jnp.bfloat16)
    outs = []
    lses = []
    for hround in range(2):
        source = source_pos[hround]
        q_blocks, k_blocks = span_keys(qk[source])
        v_plain, v_blocks = span_keys(val[source])
        output, lse = lax.map(forward_span, (q_blocks, k_blocks, v_blocks))
        outs.append(output.reshape(SEQ, D)[sort_slot[hround]])
        lses.append(lse.reshape(SEQ, HEADS)[sort_slot[hround]])
    top = jnp.maximum(lses[0], lses[1])
    total = top + jnp.log(jnp.exp(lses[0] - top) + jnp.exp(lses[1] - top))
    attended = jnp.zeros((SEQ, HEADS, HEAD_DIM), jnp.float32)
    for hround in range(2):
        share = jnp.exp(lses[hround] - total)[:, :, None]
        attended = attended + share * outs[hround].reshape(SEQ, HEADS, HEAD_DIM)
    delta = jnp.sum(out_grad.astype(jnp.float32).reshape(SEQ, HEADS, HEAD_DIM) * attended, axis=2)
    grad_x = jnp.zeros((SEQ, D), jnp.float32)
    grad_wqk = jnp.zeros((D, D), jnp.float32)
    grad_wv = jnp.zeros((D, D), jnp.float32)
    for hround in range(2):
        source = source_pos[hround]
        q_blocks, k_blocks = span_keys(qk[source])
        v_plain, v_blocks = span_keys(val[source])
        g_blocks = out_grad[source].reshape(count, SPAN, D)
        lse_blocks = total[source].reshape(count, SPAN, HEADS)
        delta_blocks = delta[source].reshape(count, SPAN, HEADS)
        grad_q, grad_k, grad_val = lax.map(backward_span, (q_blocks, k_blocks, v_blocks, g_blocks, lse_blocks, delta_blocks))
        sorted_qk = grad_q + grad_k[:, SPAN:] + jnp.roll(grad_k[:, :SPAN], -1, axis=0)
        sorted_v = grad_val[:, SPAN:] + jnp.roll(grad_val[:, :SPAN], -1, axis=0)
        grad_qk_r = sorted_qk.reshape(SEQ, D)[sort_slot[hround]].astype(jnp.bfloat16)
        grad_v_r = sorted_v.reshape(SEQ, D)[sort_slot[hround]].astype(jnp.bfloat16)
        grad_x = grad_x + jnp.dot(grad_qk_r, w_qk.T, preferred_element_type=jnp.float32)
        grad_x = grad_x + jnp.dot(grad_v_r, w_v.T, preferred_element_type=jnp.float32)
        grad_wqk = grad_wqk + jnp.dot(x2.T, grad_qk_r, preferred_element_type=jnp.float32)
        grad_wv = grad_wv + jnp.dot(x2.T, grad_v_r, preferred_element_type=jnp.float32)
    scale = SEQ ** -0.5
    return grad_x.astype(jnp.bfloat16), grad_wqk * scale, grad_wv * scale
```

```python
import functools
import math

import jax
import jax.numpy as jnp
from jax import lax
from jax.experimental import pallas as pl
from jax.experimental.pallas import tpu as pltpu
from jax.sharding import PartitionSpec as P

HEADS = 16
SPAN = 256
LAYERS = 4
PAIR = 128
BLOCK = 256
VMEM_LIMIT = 56 * 2**20
CHUNK = 64

masked_score = -1000000000.0
NT = (((1,), (1,)), ((), ()))
TN = (((0,), (0,)), ((), ()))
f32 = jnp.float32
bf16 = jnp.bfloat16


def span_ring(peers):
    side = math.isqrt(peers // LAYERS)
    if side * side * LAYERS != peers or side % 2:
        return list(range(peers))
    columns = [(0, x) for x in range(side)]
    for y in range(1, side):
        xs = range(side - 1, 0, -1) if y % 2 else range(1, side)
        columns += [(y, x) for x in xs]
    columns += [(y, 0) for y in range(side - 1, 0, -1)]
    span_of = [0] * peers
    for k, (y, x) in enumerate(columns):
        for step in range(LAYERS):
            z = step if k % 2 == 0 else LAYERS - 1 - step
            span_of[(z * side + y) * side + x] = k * LAYERS + step
    return span_of


def ordinal(group, order):
    same = group[:, None] == group[None, :]
    before = order[None, :] < order[:, None]
    return jnp.sum((same & before).astype(jnp.int32), axis=1)


def one_hot(index, total):
    return (index[:, None] == jnp.arange(total, dtype=jnp.int32)[None, :]).astype(bf16)


def mm(a, b, dims=(((1,), (0,)), ((), ()))):
    return lax.dot_general(a, b, dims, preferred_element_type=f32)


def head_masks(block):
    lane = lax.broadcasted_iota(jnp.int32, block.shape, 1)
    zero = jnp.zeros_like(block)
    low = lane < PAIR // 2
    return jnp.where(low, block, zero), jnp.where(low, zero, block)


def half_rows(block_t, h):
    row = lax.broadcasted_iota(jnp.int32, block_t.shape, 0)
    return jnp.where((row < PAIR // 2) == (h == 0), block_t, jnp.zeros_like(block_t))


def chunks():
    return [slice(k, k + CHUNK) for k in range(0, 2 * SPAN, CHUNK)]


def lanes_of(pair):
    return pl.ds(pl.multiple_of(pair * PAIR, PAIR), PAIR)


def whole_of(array):
    zeros = (0,) * len(array.shape)
    return pl.BlockSpec(array.shape, lambda i: zeros)


def params():
    return pltpu.CompilerParams(vmem_limit_bytes=VMEM_LIMIT)


def forward_kernel(scale, k_own, v_own, k_prev, v_prev, lse, inverse, out_t, kept, scores):
    step = pl.program_id(0)
    half = PAIR // 2
    rows = lax.broadcasted_iota(jnp.int32, (SPAN, SPAN), 0)
    cols = lax.broadcasted_iota(jnp.int32, (SPAN, SPAN), 1)
    for p in range(BLOCK // PAIR):
        pair = (BLOCK // PAIR) * step + p
        lanes = lanes_of(pair)
        own = k_own[:, lanes]
        vals_t = jnp.concatenate([v_prev[:, lanes].T, v_own[:, lanes].T], axis=1)
        query_t = (own.T.astype(f32) * scale).astype(bf16)
        for h in range(2):
            mine = half_rows(query_t, h)
            scores[h, :SPAN] = mm(k_prev[:, lanes], mine)
            scores[h, SPAN:] = jnp.where(rows == cols, masked_score, mm(own, mine))
        for h in range(2):
            head = pl.ds(2 * pair + h, 1)
            top = jnp.max(scores[h], axis=0, keepdims=True)
            total = jnp.zeros((8, SPAN), f32)
            for part in chunks():
                probs = jnp.exp(scores[h, part] - top)
                total += jnp.sum(probs.reshape(CHUNK // 8, 8, SPAN), axis=0)
                kept[2 * p + h, part] = probs.astype(bf16)
            total = jnp.sum(total, axis=0, keepdims=True)
            lse[head, :] = top + jnp.log(total)
            inverse[head, :] = 1.0 / total
            first = p * PAIR + h * half
            out = mm(vals_t[h * half : (h + 1) * half], kept[2 * p + h])
            out_t[first : first + half, :] = out * (1.0 / total)


def forward(k_own, v_own, k_prev, v_prev, scale):
    width = k_own.shape[1]
    heads = HEADS * BLOCK // width
    rows = pl.BlockSpec((HEADS, SPAN), lambda i: (0, 0))
    return pl.pallas_call(
        functools.partial(forward_kernel, scale),
        grid=(width // BLOCK,),
        in_specs=[whole_of(k_own)] * 4,
        out_specs=[
            rows,
            rows,
            pl.BlockSpec((BLOCK, SPAN), lambda i: (i, 0)),
            pl.BlockSpec((heads, 2 * SPAN, SPAN), lambda i: (i, 0, 0)),
        ],
        out_shape=[
            jax.ShapeDtypeStruct((HEADS, SPAN), f32),
            jax.ShapeDtypeStruct((HEADS, SPAN), f32),
            jax.ShapeDtypeStruct((width, SPAN), f32),
            jax.ShapeDtypeStruct((HEADS, 2 * SPAN, SPAN), bf16),
        ],
        scratch_shapes=[pltpu.VMEM((2, 2 * SPAN, SPAN), f32)],
        compiler_params=params(),
        name="forward",
    )(k_own, v_own, k_prev, v_prev)


def cotangent_kernel(got, pick, out_t, lse, ids, g_out, g_t, stats):
    rows = mm(pick[...], got[...])
    g_out[...] = rows.astype(bf16)
    rows_t = rows.T
    g_t[...] = rows_t.astype(bf16)
    terms = (rows_t * out_t[...]).reshape(HEADS, PAIR // 2, SPAN)
    stats[:HEADS, :] = lse[...]
    stats[HEADS : 2 * HEADS, :] = jnp.sum(terms, axis=1)
    stats[2 * HEADS :, :] = jnp.broadcast_to(ids[...], (8, SPAN))


def cotangent(got, pick, out_t, lse, ids):
    width = got.shape[1]
    whole = pl.BlockSpec(memory_space=pltpu.VMEM)
    return pl.pallas_call(
        cotangent_kernel,
        in_specs=[whole] * 5,
        out_specs=[whole] * 3,
        out_shape=[
            jax.ShapeDtypeStruct((SPAN, width), bf16),
            jax.ShapeDtypeStruct((width, SPAN), bf16),
            jax.ShapeDtypeStruct((2 * HEADS + 8, SPAN), f32),
        ],
        compiler_params=params(),
        name="cotangent",
    )(got, pick, out_t, lse, ids)


def pick_other(stats, wanted):
    group = 4
    rows = 2 * HEADS

    def body(k, acc):
        spans = [stats[group * k + j] for j in range(group)]
        values = jnp.concatenate([span[:rows] for span in spans], axis=1)
        ids = jnp.concatenate([span[rows : rows + 1] for span in spans], axis=1)
        high = values.astype(bf16)
        rest = values - high.astype(f32)
        middle = rest.astype(bf16)
        low = (rest - middle.astype(f32)).astype(bf16)
        hits = jnp.where(wanted == ids, 1.0, 0.0).astype(bf16)
        return acc + mm(jnp.concatenate([high, middle, low], axis=0), hits, NT)

    acc = lax.fori_loop(0, stats.shape[0] // group, body, jnp.zeros((3 * rows, SPAN), f32))
    return acc[:rows] + (acc[rows : 2 * rows] + acc[2 * rows :])


def backward_kernel(
    scale, stats, wanted, mine, inverse, probs, k_own, k_prev, v_own, v_prev, g_own, g_t,
    grads, factor_s, delta_s, inner_s, weight_s, dscore_s, dq_s,
):
    pair = pl.program_id(0)

    @pl.when(pair == 0)
    def _():
        other = pick_other(stats, wanted[...])
        lse_a, d_a = mine[:HEADS, :], mine[HEADS : 2 * HEADS, :]
        lse_b, d_b = other[:HEADS], other[HEADS:]
        peak = jnp.maximum(lse_a, lse_b)
        total = peak + jnp.log(jnp.exp(lse_a - peak) + jnp.exp(lse_b - peak))
        share = jnp.exp(lse_a - total)
        factor_s[...] = share * inverse[...]
        delta_s[...] = share * d_a + jnp.exp(lse_b - total) * d_b

    half = PAIR // 2
    lanes = lanes_of(pair)
    own = k_own[:, lanes]
    keys_t = jnp.concatenate([k_prev[:, lanes].T, own.T], axis=1)
    queries = head_masks((own.astype(f32) * scale).astype(bf16))
    cotangents = head_masks(g_own[:, lanes])
    for h in range(2):
        cotangent_t = half_rows(g_t[...], h)
        inner_s[h, :SPAN] = mm(v_prev[:, lanes], cotangent_t)
        inner_s[h, SPAN:] = mm(v_own[:, lanes], cotangent_t)
    for h in range(2):
        factor = factor_s[pl.ds(2 * pair + h, 1), :]
        delta = delta_s[pl.ds(2 * pair + h, 1), :]
        queried = slice(h * SPAN, (h + 1) * SPAN)
        for part in chunks():
            weight = probs[h, part].astype(f32) * factor
            weight_s[part, queried] = weight.astype(bf16)
            dscore_s[part, queried] = (weight * (inner_s[h, part] - delta)).astype(bf16)
    for h in range(2):
        part = slice(h * half, (h + 1) * half)
        dq_s[part, :] = mm(keys_t[part], dscore_s[:, h * SPAN : (h + 1) * SPAN])
    dv = mm(weight_s[...], jnp.concatenate(cotangents, axis=0))
    grads[1, :, lanes] = dv.astype(bf16)
    dk = mm(dscore_s[...], jnp.concatenate(queries, axis=0))
    grads[0, :SPAN, lanes] = dk[:SPAN].astype(bf16)
    grads[0, SPAN:, lanes] = (dk[SPAN:] + dq_s[...].T * scale).astype(bf16)


def backward(stats, wanted, mine, inverse, probs, k_own, k_prev, v_own, v_prev, g_own, g_t, scale):
    width = k_own.shape[1]
    square = pl.BlockSpec((HEADS * PAIR // width, 2 * SPAN, SPAN), lambda i: (i, 0, 0))
    out = jax.ShapeDtypeStruct((2, 2 * SPAN, width), bf16)
    return pl.pallas_call(
        functools.partial(backward_kernel, scale),
        grid=(width // PAIR,),
        in_specs=[whole_of(a) for a in (stats, wanted, mine, inverse)]
        + [square]
        + [whole_of(k_own)] * 5
        + [pl.BlockSpec((PAIR, SPAN), lambda i: (i, 0))],
        out_specs=whole_of(out),
        out_shape=out,
        scratch_shapes=[
            pltpu.VMEM((HEADS, SPAN), f32),
            pltpu.VMEM((HEADS, SPAN), f32),
            pltpu.VMEM((2, 2 * SPAN, SPAN), f32),
            pltpu.VMEM((2 * SPAN, 2 * SPAN), bf16),
            pltpu.VMEM((2 * SPAN, 2 * SPAN), bf16),
            pltpu.VMEM((PAIR, SPAN), f32),
        ],
        compiler_params=params(),
        name="backward",
    )(stats, wanted, mine, inverse, probs, k_own, k_prev, v_own, v_prev, g_own, g_t)


def combine_kernel(x_t, grads, other_k, other_v, sent):
    near, rows, width = sent.shape
    for k, other in enumerate((other_k, other_v)):
        for start in range(0, width, BLOCK):
            cols = slice(start, start + BLOCK)
            total = mm(x_t[...], grads[k, :, cols]) + other[:, cols].astype(f32)
            sent[:, k * rows // 2 : (k + 1) * rows // 2, cols] = total.reshape(
                near, rows // 2, BLOCK
            ).astype(bf16)


def combine(x_t, grads, other_k, other_v, near):
    rows, width = x_t.shape[0], grads.shape[2]
    whole = pl.BlockSpec(memory_space=pltpu.VMEM)
    return pl.pallas_call(
        combine_kernel,
        in_specs=[whole] * 4,
        out_specs=whole,
        out_shape=jax.ShapeDtypeStruct((near, 2 * rows // near, width), bf16),
        compiler_params=pltpu.CompilerParams(vmem_limit_bytes=VMEM_LIMIT // 2),
        name="combine",
    )(x_t, grads, other_k, other_v)


def place_kernel(pick_t, y_own, y_next, sent):
    rows = y_own[...].astype(f32) + y_next[...].astype(f32)
    sent[...] = mm(pick_t[...], rows.astype(bf16)).astype(bf16)


def place_rows(pick_t, y_own, y_next):
    whole = pl.BlockSpec(memory_space=pltpu.VMEM)
    return pl.pallas_call(
        place_kernel,
        in_specs=[whole] * 3,
        out_specs=whole,
        out_shape=jax.ShapeDtypeStruct((pick_t.shape[0], y_own.shape[1]), bf16),
        compiler_params=params(),
        name="place_rows",
    )(pick_t, y_own, y_next)


def per_device(x2, out_grad, w_qk, w_v, sort_slot, source_pos):
    tdev, width = x2.shape
    part_rows = tdev // 2
    peers = lax.axis_size("ctx")
    near = peers // 2
    cap = 2 * tdev // peers
    slots = 2 * near * cap
    scale = (width // HEADS) ** (-0.5)
    chip = lax.axis_index("ctx")
    hround = lax.axis_index("round")
    side = chip // near
    both = ("ctx", "round")

    ring = span_ring(peers)
    span_of = [ring, [(peers - m) % peers for m in ring]]
    holder = [[spans.index(m) for m in range(peers)] for spans in span_of]

    def flat(c, r):
        return 2 * c + r

    every = [(c, r) for c in range(peers) for r in range(2)]
    onward = [
        (flat(holder[r][m], r), flat(holder[r][(m + 1) % peers], r))
        for m in range(peers)
        for r in range(2)
    ]
    backward_way = [(b, a) for a, b in onward]
    fetch = [(flat(span_of[r][c], r), flat(c, r)) for c, r in every]
    mirror = [(flat(c, r), flat((c + near) % peers, r)) for c, r in every]
    swap = [(flat(c, r), flat(c, 1 - r)) for c, r in every]
    swap_mirror = [(flat(c, r), flat((c + near) % peers, 1 - r)) for c, r in every]
    halves = [list(range(near)), list(range(near, peers))]

    def move(rows, route):
        return lax.ppermute(rows, both, route)

    def exchange(blocks):
        return lax.all_to_all(blocks, "ctx", 0, 0, axis_index_groups=halves, tiled=True)

    def my_part(rows):
        return lax.dynamic_slice_in_dim(rows, hround * part_rows, part_rows, 0)

    def their_part(rows):
        return lax.dynamic_slice_in_dim(rows, (1 - hround) * part_rows, part_rows, 0)

    own_spans = lax.dynamic_index_in_dim(sort_slot, hround, 0, keepdims=False) // SPAN
    spare = jnp.zeros((16, width - tdev), bf16)
    label = jnp.broadcast_to(own_spans.astype(bf16)[None, :], (16, tdev))
    label = jnp.concatenate([label, spare], axis=1)
    far_x = move(jnp.concatenate([my_part(x2), label], axis=0), mirror)
    far_x, half_g = lax.optimization_barrier((far_x, my_part(out_grad)))
    far_g = move(half_g, mirror)
    far_spans = far_x[part_rows, :tdev].astype(jnp.int32)
    far_x = far_x[:part_rows]

    def send_index(spans):
        tables = jnp.where(
            hround == 0, jnp.array(span_of[0], jnp.int32), jnp.array(span_of[1], jnp.int32)
        )
        held = spans[:, None] == tables[None, :]
        owner = jnp.sum(jnp.where(held, jnp.arange(peers, dtype=jnp.int32)[None, :], 0), axis=1)
        order = ordinal(owner, jnp.arange(tdev, dtype=jnp.int32))
        return jnp.where(owner // near == side, owner % near, peers) * 2 * cap + order

    near_index = send_index(own_spans)
    far_index = send_index(far_spans) + cap
    rolled = jnp.where(hround == 0, far_index, jnp.roll(far_index, part_rows, axis=0))
    send = one_hot(near_index, slots)
    send_far = one_hot(far_index, slots)
    send_far_rolled = one_hot(rolled, slots)
    sources = move(source_pos[0], fetch)
    group = sources // tdev
    is_near = group // near == side
    place = 2 * (group % near) * cap + jnp.where(is_near, 0, cap) + ordinal(group, sources)
    pick = one_hot(place, slots)

    def in_slots(rows, far_rows):
        far_rows = jnp.concatenate([far_rows, move(far_rows, swap)], axis=0)
        sent = mm(send, rows, TN) + mm(send_far_rolled, far_rows, TN)
        return sent.astype(bf16).reshape(near, 2 * cap, width)

    sent_x, sources = lax.optimization_barrier((in_slots(x2, far_x), sources))
    got_x = exchange(sent_x).reshape(slots, width)
    x_own = mm(pick, got_x).astype(bf16)
    x_prev = move(x_own, onward)
    far_g, _ = lax.optimization_barrier((far_g, x_own))
    k_own = mm(x_own, w_qk).astype(bf16)
    v_own = mm(x_own, w_v).astype(bf16)

    sent_g = in_slots(out_grad, far_g)
    x_prev, k_own, v_own, sent_g = lax.optimization_barrier((x_prev, k_own, v_own, sent_g))
    got_g = exchange(sent_g).reshape(slots, width)
    k_prev = mm(x_prev, w_qk).astype(bf16)
    v_prev = mm(x_prev, w_v).astype(bf16)
    lse, inverse, out_t, probs = forward(k_own, v_own, k_prev, v_prev, scale)
    ids = sources.astype(f32)
    g_own, g_t, mine = cotangent(got_g, pick, out_t, lse, ids[None, :])

    told = jnp.stack([move(mine, swap), move(mine, swap_mirror)])
    stats = exchange(jnp.broadcast_to(told[None], (near,) + told.shape))
    stats = stats.reshape((peers,) + mine.shape)
    grads = backward(
        stats, ids[:, None], mine, inverse, probs, k_own, k_prev, v_own, v_prev, g_own, g_t, scale
    )

    y_prev = (mm(grads[0, :SPAN], w_qk, NT) + mm(grads[1, :SPAN], w_v, NT)).astype(bf16)
    y_next = move(y_prev, backward_way)

    each = width // (2 * peers)
    spot = jnp.arange(near * each, dtype=jnp.int32)
    x_both = jnp.concatenate([x_prev, x_own], axis=0)

    def columns_for(core, half):
        column = (half * near + spot // each) * (2 * each) + core * each + spot % each
        ordered = jnp.arange(width, dtype=jnp.int32)[None, :] == column[:, None]
        return mm(ordered.astype(bf16), x_both, NT).astype(bf16)

    def weight_terms(half, after):
        x_ours, x_theirs = columns_for(hround, half), columns_for(1 - hround, half)
        x_theirs, _ = lax.optimization_barrier((x_theirs, after))
        theirs = [move(mm(x_theirs, grads[k]).astype(bf16), swap) for k in range(2)]
        return combine(x_ours, grads, theirs[0], theirs[1], near)

    y_own = (mm(grads[0, SPAN:], w_qk, NT) + mm(grads[1, SPAN:], w_v, NT)).astype(bf16)
    sent_y = place_rows(jnp.transpose(pick), y_own, y_next).reshape(near, 2 * cap, width)
    got_y = exchange(sent_y)
    terms, got_y = lax.optimization_barrier((weight_terms(1 - side, y_prev), got_y))
    got_far_w = exchange(terms)
    terms, got_far_w = lax.optimization_barrier((weight_terms(side, sent_y), got_far_w))
    got_w = exchange(terms)

    got_y = got_y.reshape(slots, width)
    rows_far = mm(send_far, got_y)
    rows_near = mm(send, got_y)
    from_core = jnp.concatenate([their_part(rows_far), their_part(rows_near)], axis=0)
    from_core = move(from_core.astype(bf16), swap).astype(f32)
    crossing = move((my_part(rows_far) + from_core[:part_rows]).astype(bf16), mirror)
    grad_x = (my_part(rows_near) + from_core[part_rows:] + crossing.astype(f32)).astype(bf16)
    crossing_w = move(jnp.sum(got_far_w.astype(f32), axis=0).astype(bf16), mirror)

    got_w, grad_x, crossing_w = lax.optimization_barrier((got_w, grad_x, crossing_w))
    weight_grads = jnp.sum(got_w.astype(f32), axis=0) + crossing_w.astype(f32)
    weight_grads = weight_grads * (tdev * peers) ** (-0.5)
    return (grad_x, weight_grads[:each], weight_grads[each:])


def solution(mesh):
    placed = (P("ctx", None), P("ctx", None), P(), P(), P(None, "ctx"), P("round", "ctx"))
    return jax.shard_map(
        per_device,
        mesh=mesh,
        in_specs=placed,
        out_specs=(P(("ctx", "round"), None), P(("ctx", "round"), None), P(("ctx", "round"), None)),
        check_vma=False,
    )
```

```python
import functools
import math

import jax
import jax.numpy as jnp
from jax import lax
from jax.experimental import pallas as pl
from jax.experimental.pallas import tpu as pltpu
from jax.sharding import PartitionSpec as P

HEADS = 16
SPAN = 256
LAYERS = 4
PAIR = 128
BLOCK = 256
VMEM_LIMIT = 56 * 2**20
CHUNK = 64

masked_score = -1000000000.0
NT = (((1,), (1,)), ((), ()))
TN = (((0,), (0,)), ((), ()))
f32 = jnp.float32
bf16 = jnp.bfloat16


def span_ring(peers):
    side = math.isqrt(peers // LAYERS)
    if side * side * LAYERS != peers or side % 2:
        return list(range(peers))
    columns = [(0, x) for x in range(side)]
    for y in range(1, side):
        xs = range(side - 1, 0, -1) if y % 2 else range(1, side)
        columns += [(y, x) for x in xs]
    columns += [(y, 0) for y in range(side - 1, 0, -1)]
    span_of = [0] * peers
    for k, (y, x) in enumerate(columns):
        for step in range(LAYERS):
            z = step if k % 2 == 0 else LAYERS - 1 - step
            span_of[(z * side + y) * side + x] = k * LAYERS + step
    return span_of


def ordinal(group, order):
    same = group[:, None] == group[None, :]
    before = order[None, :] < order[:, None]
    return jnp.sum((same & before).astype(jnp.int32), axis=1)


def one_hot(index, total):
    return (index[:, None] == jnp.arange(total, dtype=jnp.int32)[None, :]).astype(bf16)


def mm(a, b, dims=(((1,), (0,)), ((), ()))):
    return lax.dot_general(a, b, dims, preferred_element_type=f32)


def head_masks(block):
    lane = lax.broadcasted_iota(jnp.int32, block.shape, 1)
    zero = jnp.zeros_like(block)
    low = lane < PAIR // 2
    return jnp.where(low, block, zero), jnp.where(low, zero, block)


def half_rows(block_t, h):
    row = lax.broadcasted_iota(jnp.int32, block_t.shape, 0)
    return jnp.where((row < PAIR // 2) == (h == 0), block_t, jnp.zeros_like(block_t))


def chunks():
    return [slice(k, k + CHUNK) for k in range(0, 2 * SPAN, CHUNK)]


def lanes_of(pair):
    return pl.ds(pl.multiple_of(pair * PAIR, PAIR), PAIR)


def whole_of(array):
    zeros = (0,) * len(array.shape)
    return pl.BlockSpec(array.shape, lambda i: zeros)


def params():
    return pltpu.CompilerParams(vmem_limit_bytes=VMEM_LIMIT)


def forward_kernel(scale, k_own, v_own, k_prev, v_prev, lse, inverse, out_t, kept, scores):
    step = pl.program_id(0)
    half = PAIR // 2
    rows = lax.broadcasted_iota(jnp.int32, (SPAN, SPAN), 0)
    cols = lax.broadcasted_iota(jnp.int32, (SPAN, SPAN), 1)
    for p in range(BLOCK // PAIR):
        pair = (BLOCK // PAIR) * step + p
        lanes = lanes_of(pair)
        own = k_own[:, lanes]
        vals_t = jnp.concatenate([v_prev[:, lanes].T, v_own[:, lanes].T], axis=1)
        query_t = (own.T.astype(f32) * scale).astype(bf16)
        for h in range(2):
            mine = half_rows(query_t, h)
            scores[h, :SPAN] = mm(k_prev[:, lanes], mine)
            scores[h, SPAN:] = jnp.where(rows == cols, masked_score, mm(own, mine))
        for h in range(2):
            head = pl.ds(2 * pair + h, 1)
            top = jnp.max(scores[h], axis=0, keepdims=True)
            total = jnp.zeros((8, SPAN), f32)
            for part in chunks():
                probs = jnp.exp(scores[h, part] - top)
                total += jnp.sum(probs.reshape(CHUNK // 8, 8, SPAN), axis=0)
                kept[2 * p + h, part] = probs.astype(bf16)
            total = jnp.sum(total, axis=0, keepdims=True)
            lse[head, :] = top + jnp.log(total)
            inverse[head, :] = 1.0 / total
            first = p * PAIR + h * half
            out = mm(vals_t[h * half : (h + 1) * half], kept[2 * p + h])
            out_t[first : first + half, :] = out * (1.0 / total)


def forward(k_own, v_own, k_prev, v_prev, scale):
    width = k_own.shape[1]
    heads = HEADS * BLOCK // width
    rows = pl.BlockSpec((HEADS, SPAN), lambda i: (0, 0))
    return pl.pallas_call(
        functools.partial(forward_kernel, scale),
        grid=(width // BLOCK,),
        in_specs=[whole_of(k_own)] * 4,
        out_specs=[
            rows,
            rows,
            pl.BlockSpec((BLOCK, SPAN), lambda i: (i, 0)),
            pl.BlockSpec((heads, 2 * SPAN, SPAN), lambda i: (i, 0, 0)),
        ],
        out_shape=[
            jax.ShapeDtypeStruct((HEADS, SPAN), f32),
            jax.ShapeDtypeStruct((HEADS, SPAN), f32),
            jax.ShapeDtypeStruct((width, SPAN), f32),
            jax.ShapeDtypeStruct((HEADS, 2 * SPAN, SPAN), bf16),
        ],
        scratch_shapes=[pltpu.VMEM((2, 2 * SPAN, SPAN), f32)],
        compiler_params=params(),
        name="forward",
    )(k_own, v_own, k_prev, v_prev)


def cotangent_kernel(got, pick, out_t, lse, ids, g_out, g_t, stats):
    rows = mm(pick[...], got[...])
    g_out[...] = rows.astype(bf16)
    rows_t = rows.T
    g_t[...] = rows_t.astype(bf16)
    terms = (rows_t * out_t[...]).reshape(HEADS, PAIR // 2, SPAN)
    stats[:HEADS, :] = lse[...]
    stats[HEADS : 2 * HEADS, :] = jnp.sum(terms, axis=1)
    stats[2 * HEADS :, :] = jnp.broadcast_to(ids[...], (8, SPAN))


def cotangent(got, pick, out_t, lse, ids):
    width = got.shape[1]
    whole = pl.BlockSpec(memory_space=pltpu.VMEM)
    return pl.pallas_call(
        cotangent_kernel,
        in_specs=[whole] * 5,
        out_specs=[whole] * 3,
        out_shape=[
            jax.ShapeDtypeStruct((SPAN, width), bf16),
            jax.ShapeDtypeStruct((width, SPAN), bf16),
            jax.ShapeDtypeStruct((2 * HEADS + 8, SPAN), f32),
        ],
        compiler_params=params(),
        name="cotangent",
    )(got, pick, out_t, lse, ids)


def pick_other(stats, wanted):
    group = 4
    rows = 2 * HEADS

    def body(k, acc):
        spans = [stats[group * k + j] for j in range(group)]
        values = jnp.concatenate([span[:rows] for span in spans], axis=1)
        ids = jnp.concatenate([span[rows : rows + 1] for span in spans], axis=1)
        high = values.astype(bf16)
        rest = values - high.astype(f32)
        middle = rest.astype(bf16)
        low = (rest - middle.astype(f32)).astype(bf16)
        hits = jnp.where(wanted == ids, 1.0, 0.0).astype(bf16)
        return acc + mm(jnp.concatenate([high, middle, low], axis=0), hits, NT)

    acc = lax.fori_loop(0, stats.shape[0] // group, body, jnp.zeros((3 * rows, SPAN), f32))
    return acc[:rows] + (acc[rows : 2 * rows] + acc[2 * rows :])


def backward_kernel(
    scale, stats, wanted, mine, inverse, probs, k_own, k_prev, v_own, v_prev, g_own, g_t,
    grads, factor_s, delta_s, inner_s, weight_s, dscore_s, dq_s,
):
    step = pl.program_id(0)

    @pl.when(step == 0)
    def _():
        other = pick_other(stats, wanted[...])
        lse_a, d_a = mine[:HEADS, :], mine[HEADS : 2 * HEADS, :]
        lse_b, d_b = other[:HEADS], other[HEADS:]
        peak = jnp.maximum(lse_a, lse_b)
        total = peak + jnp.log(jnp.exp(lse_a - peak) + jnp.exp(lse_b - peak))
        share = jnp.exp(lse_a - total)
        factor_s[...] = share * inverse[...]
        delta_s[...] = share * d_a + jnp.exp(lse_b - total) * d_b

    half = PAIR // 2
    for p in range(BLOCK // PAIR):
        pair = (BLOCK // PAIR) * step + p
        lanes = lanes_of(pair)
        own = k_own[:, lanes]
        keys_t = jnp.concatenate([k_prev[:, lanes].T, own.T], axis=1)
        queries = head_masks((own.astype(f32) * scale).astype(bf16))
        cotangents = head_masks(g_own[:, lanes])
        for h in range(2):
            cotangent_t = half_rows(g_t[p * PAIR : (p + 1) * PAIR, :], h)
            inner_s[p, h, :SPAN] = mm(v_prev[:, lanes], cotangent_t)
            inner_s[p, h, SPAN:] = mm(v_own[:, lanes], cotangent_t)
        for h in range(2):
            factor = factor_s[pl.ds(2 * pair + h, 1), :]
            delta = delta_s[pl.ds(2 * pair + h, 1), :]
            queried = slice(h * SPAN, (h + 1) * SPAN)
            for part in chunks():
                weight = probs[2 * p + h, part].astype(f32) * factor
                weight_s[p, part, queried] = weight.astype(bf16)
                dscore_s[p, part, queried] = (weight * (inner_s[p, h, part] - delta)).astype(bf16)
        for h in range(2):
            part = slice(h * half, (h + 1) * half)
            dq_s[p, part, :] = mm(keys_t[part], dscore_s[p, :, h * SPAN : (h + 1) * SPAN])
        dv = mm(weight_s[p], jnp.concatenate(cotangents, axis=0))
        grads[1, :, lanes] = dv.astype(bf16)
        dk = mm(dscore_s[p], jnp.concatenate(queries, axis=0))
        grads[0, :SPAN, lanes] = dk[:SPAN].astype(bf16)
        grads[0, SPAN:, lanes] = (dk[SPAN:] + dq_s[p].T * scale).astype(bf16)


def backward(stats, wanted, mine, inverse, probs, k_own, k_prev, v_own, v_prev, g_own, g_t, scale):
    width = k_own.shape[1]
    square = pl.BlockSpec((HEADS * BLOCK // width, 2 * SPAN, SPAN), lambda i: (i, 0, 0))
    out = jax.ShapeDtypeStruct((2, 2 * SPAN, width), bf16)
    return pl.pallas_call(
        functools.partial(backward_kernel, scale),
        grid=(width // BLOCK,),
        in_specs=[whole_of(a) for a in (stats, wanted, mine, inverse)]
        + [square]
        + [whole_of(k_own)] * 5
        + [pl.BlockSpec((BLOCK, SPAN), lambda i: (i, 0))],
        out_specs=whole_of(out),
        out_shape=out,
        scratch_shapes=[
            pltpu.VMEM((HEADS, SPAN), f32),
            pltpu.VMEM((HEADS, SPAN), f32),
            pltpu.VMEM((BLOCK // PAIR, 2, 2 * SPAN, SPAN), f32),
            pltpu.VMEM((BLOCK // PAIR, 2 * SPAN, 2 * SPAN), bf16),
            pltpu.VMEM((BLOCK // PAIR, 2 * SPAN, 2 * SPAN), bf16),
            pltpu.VMEM((BLOCK // PAIR, PAIR, SPAN), f32),
        ],
        compiler_params=params(),
        name="backward",
    )(stats, wanted, mine, inverse, probs, k_own, k_prev, v_own, v_prev, g_own, g_t)


def small_params():
    return pltpu.CompilerParams(vmem_limit_bytes=VMEM_LIMIT // 4)


def cut_rows(total, low, leave, keep, cols):
    rows, width = total.shape
    cut = total.reshape(rows // (2 * low), 2, low, width)
    leave[:, cols] = cut[:, 1].reshape(rows // 2, width).astype(bf16)
    keep[:, cols] = cut[:, 0].reshape(rows // 2, width).astype(bf16)


def first_fold_kernel(edges, lows, x_t, grads, other_k, other_v, *outs):
    width = grads.shape[2]
    for part, low in enumerate(lows):
        for start in range(edges[part], edges[part + 1], BLOCK):
            kind, cols = start // width, slice(start % width, start % width + BLOCK)
            other = (other_k, other_v)[kind]
            total = mm(x_t[...], grads[kind, :, cols]) + other[:, cols].astype(f32)
            inside = slice(start - edges[part], start - edges[part] + BLOCK)
            cut_rows(total, low, outs[2 * part], outs[2 * part + 1], inside)


def fold_kernel(lows, *refs):
    outs = refs[2 * len(lows) :]
    for k, low in enumerate(lows):
        total = refs[2 * k][...].astype(f32) + refs[2 * k + 1][...].astype(f32)
        cut_rows(total, low, outs[2 * k], outs[2 * k + 1], slice(0, total.shape[1]))


def call_fold(kernel, operands, rows, widths, name):
    shapes = [jax.ShapeDtypeStruct((rows, w), bf16) for w in widths for _ in range(2)]
    whole = pl.BlockSpec(memory_space=pltpu.VMEM)
    outs = pl.pallas_call(
        kernel,
        in_specs=[whole] * len(operands),
        out_specs=[whole] * len(shapes),
        out_shape=shapes,
        compiler_params=small_params(),
        name=name,
    )(*operands)
    return [(outs[2 * k], outs[2 * k + 1]) for k in range(len(widths))]


def place_kernel(pick_t, y_own, y_next, sent):
    rows = y_own[...].astype(f32) + y_next[...].astype(f32)
    sent[...] = mm(pick_t[...], rows.astype(bf16)).astype(bf16)


def place_rows(pick_t, y_own, y_next):
    whole = pl.BlockSpec(memory_space=pltpu.VMEM)
    return pl.pallas_call(
        place_kernel,
        in_specs=[whole] * 3,
        out_specs=whole,
        out_shape=jax.ShapeDtypeStruct((pick_t.shape[0], y_own.shape[1]), bf16),
        compiler_params=small_params(),
        name="place_rows",
    )(pick_t, y_own, y_next)


def per_device(x2, out_grad, w_qk, w_v, sort_slot, source_pos):
    tdev, width = x2.shape
    part_rows = tdev // 2
    peers = lax.axis_size("ctx")
    near = peers // 2
    cap = 2 * tdev // peers
    slots = 2 * near * cap
    scale = (width // HEADS) ** (-0.5)
    chip = lax.axis_index("ctx")
    hround = lax.axis_index("round")
    side = chip // near
    both = ("ctx", "round")

    ring = span_ring(peers)
    span_of = [ring, [(peers - m) % peers for m in ring]]
    holder = [[spans.index(m) for m in range(peers)] for spans in span_of]

    def flat(c, r):
        return 2 * c + r

    every = [(c, r) for c in range(peers) for r in range(2)]
    onward = [
        (flat(holder[r][m], r), flat(holder[r][(m + 1) % peers], r))
        for m in range(peers)
        for r in range(2)
    ]
    backward_way = [(b, a) for a, b in onward]
    fetch = [(flat(span_of[r][c], r), flat(c, r)) for c, r in every]
    mirror = [(flat(c, r), flat((c + near) % peers, r)) for c, r in every]
    swap = [(flat(c, r), flat(c, 1 - r)) for c, r in every]
    swap_mirror = [(flat(c, r), flat((c + near) % peers, 1 - r)) for c, r in every]
    halves = [list(range(near)), list(range(near, peers))]

    def move(rows, route):
        return lax.ppermute(rows, both, route)

    def exchange(blocks):
        return lax.all_to_all(blocks, "ctx", 0, 0, axis_index_groups=halves, tiled=True)

    def my_part(rows):
        return lax.dynamic_slice_in_dim(rows, hround * part_rows, part_rows, 0)

    def their_part(rows):
        return lax.dynamic_slice_in_dim(rows, (1 - hround) * part_rows, part_rows, 0)

    own_spans = lax.dynamic_index_in_dim(sort_slot, hround, 0, keepdims=False) // SPAN
    spare = jnp.zeros((16, width - tdev), bf16)
    label = jnp.broadcast_to(own_spans.astype(bf16)[None, :], (16, tdev))
    label = jnp.concatenate([label, spare], axis=1)
    far_x = move(jnp.concatenate([my_part(x2), label], axis=0), mirror)
    far_x, half_g = lax.optimization_barrier((far_x, my_part(out_grad)))
    far_g = move(half_g, mirror)
    far_spans = far_x[part_rows, :tdev].astype(jnp.int32)
    far_x = far_x[:part_rows]

    def send_index(spans):
        tables = jnp.where(
            hround == 0, jnp.array(span_of[0], jnp.int32), jnp.array(span_of[1], jnp.int32)
        )
        held = spans[:, None] == tables[None, :]
        owner = jnp.sum(jnp.where(held, jnp.arange(peers, dtype=jnp.int32)[None, :], 0), axis=1)
        order = ordinal(owner, jnp.arange(tdev, dtype=jnp.int32))
        return jnp.where(owner // near == side, owner % near, peers) * 2 * cap + order

    near_index = send_index(own_spans)
    far_index = send_index(far_spans) + cap
    rolled = jnp.where(hround == 0, far_index, jnp.roll(far_index, part_rows, axis=0))
    send = one_hot(near_index, slots)
    send_far = one_hot(far_index, slots)
    send_far_rolled = one_hot(rolled, slots)
    sources = move(source_pos[0], fetch)
    group = sources // tdev
    is_near = group // near == side
    place = 2 * (group % near) * cap + jnp.where(is_near, 0, cap) + ordinal(group, sources)
    pick = one_hot(place, slots)

    def in_slots(rows, far_rows):
        far_rows = jnp.concatenate([far_rows, move(far_rows, swap)], axis=0)
        sent = mm(send, rows, TN) + mm(send_far_rolled, far_rows, TN)
        return sent.astype(bf16).reshape(near, 2 * cap, width)

    sent_x, sources = lax.optimization_barrier((in_slots(x2, far_x), sources))
    got_x = exchange(sent_x).reshape(slots, width)
    x_own = mm(pick, got_x).astype(bf16)
    x_prev = move(x_own, onward)
    far_g, _ = lax.optimization_barrier((far_g, x_own))
    k_own = mm(x_own, w_qk).astype(bf16)
    v_own = mm(x_own, w_v).astype(bf16)

    sent_g = in_slots(out_grad, far_g)
    x_prev, k_own, v_own, sent_g = lax.optimization_barrier((x_prev, k_own, v_own, sent_g))
    got_g = exchange(sent_g).reshape(slots, width)
    k_prev = mm(x_prev, w_qk).astype(bf16)
    v_prev = mm(x_prev, w_v).astype(bf16)
    lse, inverse, out_t, probs = forward(k_own, v_own, k_prev, v_prev, scale)
    ids = sources.astype(f32)
    g_own, g_t, mine = cotangent(got_g, pick, out_t, lse, ids[None, :])

    told = jnp.stack([move(mine, swap), move(mine, swap_mirror)])
    stats = exchange(jnp.broadcast_to(told[None], (near,) + told.shape))
    stats = stats.reshape((peers,) + mine.shape)

    each = width // (2 * peers)
    spot = jnp.arange(width // 2, dtype=jnp.int32)
    column = ((spot // each) ^ chip) * (2 * each) + spot % each
    x_both = jnp.concatenate([x_prev, x_own], axis=0)

    def columns_for(core):
        ordered = jnp.arange(width, dtype=jnp.int32)[None, :] == (column + core * each)[:, None]
        return mm(ordered.astype(bf16), x_both, NT).astype(bf16)

    x_ours, x_theirs = columns_for(hround), columns_for(1 - hround)
    stats, x_ours, x_theirs = lax.optimization_barrier((stats, x_ours, x_theirs))
    grads = backward(
        stats, ids[:, None], mine, inverse, probs, k_own, k_prev, v_own, v_prev, g_own, g_t, scale
    )

    y_prev = (mm(grads[0, :SPAN], w_qk, NT) + mm(grads[1, :SPAN], w_v, NT)).astype(bf16)
    y_next = move(y_prev, backward_way)

    x_theirs, _ = lax.optimization_barrier((x_theirs, y_prev))
    theirs = [move(mm(x_theirs, grads[k]).astype(bf16), swap) for k in range(2)]
    y_own = (mm(grads[0, SPAN:], w_qk, NT) + mm(grads[1, SPAN:], w_v, NT)).astype(bf16)

    bits = near.bit_length() - 1
    blocks = 2 * width // BLOCK
    edges = [BLOCK * ((blocks * k + 2) // 3) for k in range(4)]
    widths = [edges[k + 1] - edges[k] for k in range(3)]
    left = [list(range(bits + 1)) for _ in range(3)]
    pairs = None
    for turn in range(bits):
        turn_bits = [(k * bits // 3 + turn) % bits for k in range(3)]
        lows = [each << left[k].index(bit) for k, bit in enumerate(turn_bits)]
        if turn == 0:
            kernel = functools.partial(first_fold_kernel, edges, lows)
            operands = [x_ours, grads, theirs[0], theirs[1]]
        else:
            kernel = functools.partial(fold_kernel, lows)
            operands = [array for pair in pairs for array in pair]
        cuts = call_fold(kernel, operands, (width // 2) >> (turn + 1), widths, "fold")
        if turn == 0:
            y_next, cuts = lax.optimization_barrier((y_next, cuts))
            sent_y = place_rows(jnp.transpose(pick), y_own, y_next)
            got_y = exchange(sent_y.reshape(near, 2 * cap, width)).reshape(slots, width)
        if turn == 1:
            got_y, cuts = lax.optimization_barrier((got_y, cuts))
            rows_far = mm(send_far, got_y)
            rows_near = mm(send, got_y)
            from_core = jnp.concatenate([their_part(rows_far), their_part(rows_near)], axis=0)
            from_core = move(from_core.astype(bf16), swap)
        pairs = []
        for k, (leave, keep) in enumerate(cuts):
            left[k].remove(turn_bits[k])
            route = [(flat(c, r), flat(c ^ (1 << turn_bits[k]), r)) for c, r in every]
            pairs.append((keep, move(leave, route)))
        if turn == 1:
            pairs, from_core = lax.optimization_barrier((pairs, from_core))
            from_core = from_core.astype(f32)
            crossing = move((my_part(rows_far) + from_core[:part_rows]).astype(bf16), mirror)
            grad_x = my_part(rows_near) + from_core[part_rows:] + crossing.astype(f32)
            grad_x = grad_x.astype(bf16)

    pairs, grad_x = lax.optimization_barrier((pairs, grad_x))
    summed = jnp.concatenate([a.astype(f32) + b.astype(f32) for a, b in pairs], axis=1)
    leaving = move(summed[each:].astype(bf16), mirror).astype(f32)
    weight_grads = (summed[:each] + leaving) * (tdev * peers) ** (-0.5)
    return (grad_x, weight_grads[:, :width], weight_grads[:, width:])


def solution(mesh):
    placed = (P("ctx", None), P("ctx", None), P(), P(), P(None, "ctx"), P("round", "ctx"))
    return jax.shard_map(
        per_device,
        mesh=mesh,
        in_specs=placed,
        out_specs=(P(("ctx", "round"), None), P(("ctx", "round"), None), P(("ctx", "round"), None)),
        check_vma=False,
    )
```

```python
import functools
import math

import jax
import jax.numpy as jnp
from jax import lax
from jax.experimental import pallas as pl
from jax.experimental.pallas import tpu as pltpu
from jax.sharding import PartitionSpec as P

HEADS = 16
SPAN = 256
LAYERS = 4
PAIR = 128
BLOCK = 256
VMEM_LIMIT = 56 * 2**20
CHUNK = 64

masked_score = -1000000000.0
NT = (((1,), (1,)), ((), ()))
TN = (((0,), (0,)), ((), ()))
f32 = jnp.float32
bf16 = jnp.bfloat16


def span_ring(peers):
    side = math.isqrt(peers // LAYERS)
    if side * side * LAYERS != peers or side % 2:
        return list(range(peers))
    columns = [(0, x) for x in range(side)]
    for y in range(1, side):
        xs = range(side - 1, 0, -1) if y % 2 else range(1, side)
        columns += [(y, x) for x in xs]
    columns += [(y, 0) for y in range(side - 1, 0, -1)]
    span_of = [0] * peers
    for k, (y, x) in enumerate(columns):
        for step in range(LAYERS):
            z = step if k % 2 == 0 else LAYERS - 1 - step
            span_of[(z * side + y) * side + x] = k * LAYERS + step
    return span_of


def ordinal(group, order):
    same = group[:, None] == group[None, :]
    before = order[None, :] < order[:, None]
    return jnp.sum((same & before).astype(jnp.int32), axis=1)


def one_hot(index, total):
    return (index[:, None] == jnp.arange(total, dtype=jnp.int32)[None, :]).astype(bf16)


def mm(a, b, dims=(((1,), (0,)), ((), ()))):
    return lax.dot_general(a, b, dims, preferred_element_type=f32)


def head_masks(block):
    lane = lax.broadcasted_iota(jnp.int32, block.shape, 1)
    zero = jnp.zeros_like(block)
    low = lane < PAIR // 2
    return jnp.where(low, block, zero), jnp.where(low, zero, block)


def half_rows(block_t, h):
    row = lax.broadcasted_iota(jnp.int32, block_t.shape, 0)
    return jnp.where((row < PAIR // 2) == (h == 0), block_t, jnp.zeros_like(block_t))


def chunks():
    return [slice(k, k + CHUNK) for k in range(0, 2 * SPAN, CHUNK)]


def lanes_of(pair):
    return pl.ds(pl.multiple_of(pair * PAIR, PAIR), PAIR)


def whole_of(array):
    zeros = (0,) * len(array.shape)
    return pl.BlockSpec(array.shape, lambda i: zeros)


def params():
    return pltpu.CompilerParams(vmem_limit_bytes=VMEM_LIMIT)


def forward_kernel(scale, k_own, v_own, k_prev, v_prev, lse, inverse, out_t, kept, scores):
    step = pl.program_id(0)
    half = PAIR // 2
    rows = lax.broadcasted_iota(jnp.int32, (SPAN, SPAN), 0)
    cols = lax.broadcasted_iota(jnp.int32, (SPAN, SPAN), 1)
    for p in range(BLOCK // PAIR):
        pair = (BLOCK // PAIR) * step + p
        lanes = lanes_of(pair)
        own = k_own[:, lanes]
        vals_t = jnp.concatenate([v_prev[:, lanes].T, v_own[:, lanes].T], axis=1)
        query_t = (own.T.astype(f32) * scale).astype(bf16)
        for h in range(2):
            mine = half_rows(query_t, h)
            scores[h, :SPAN] = mm(k_prev[:, lanes], mine)
            scores[h, SPAN:] = jnp.where(rows == cols, masked_score, mm(own, mine))
        for h in range(2):
            head = pl.ds(2 * pair + h, 1)
            top = jnp.max(scores[h], axis=0, keepdims=True)
            total = jnp.zeros((8, SPAN), f32)
            for part in chunks():
                probs = jnp.exp(scores[h, part] - top)
                total += jnp.sum(probs.reshape(CHUNK // 8, 8, SPAN), axis=0)
                kept[2 * p + h, part] = probs.astype(bf16)
            total = jnp.sum(total, axis=0, keepdims=True)
            lse[head, :] = top + jnp.log(total)
            inverse[head, :] = 1.0 / total
            first = p * PAIR + h * half
            out = mm(vals_t[h * half : (h + 1) * half], kept[2 * p + h])
            out_t[first : first + half, :] = out * (1.0 / total)


def forward(k_own, v_own, k_prev, v_prev, scale):
    width = k_own.shape[1]
    heads = HEADS * BLOCK // width
    rows = pl.BlockSpec((HEADS, SPAN), lambda i: (0, 0))
    return pl.pallas_call(
        functools.partial(forward_kernel, scale),
        grid=(width // BLOCK,),
        in_specs=[whole_of(k_own)] * 4,
        out_specs=[
            rows,
            rows,
            pl.BlockSpec((BLOCK, SPAN), lambda i: (i, 0)),
            pl.BlockSpec((heads, 2 * SPAN, SPAN), lambda i: (i, 0, 0)),
        ],
        out_shape=[
            jax.ShapeDtypeStruct((HEADS, SPAN), f32),
            jax.ShapeDtypeStruct((HEADS, SPAN), f32),
            jax.ShapeDtypeStruct((width, SPAN), f32),
            jax.ShapeDtypeStruct((HEADS, 2 * SPAN, SPAN), bf16),
        ],
        scratch_shapes=[pltpu.VMEM((2, 2 * SPAN, SPAN), f32)],
        compiler_params=params(),
        name="forward",
    )(k_own, v_own, k_prev, v_prev)


def cotangent_kernel(got, pick, out_t, lse, ids, g_out, g_t, stats):
    rows = mm(pick[...], got[...])
    g_out[...] = rows.astype(bf16)
    rows_t = rows.T
    g_t[...] = rows_t.astype(bf16)
    terms = (rows_t * out_t[...]).reshape(HEADS, PAIR // 2, SPAN)
    stats[:HEADS, :] = lse[...]
    stats[HEADS : 2 * HEADS, :] = jnp.sum(terms, axis=1)
    stats[2 * HEADS :, :] = jnp.broadcast_to(ids[...], (8, SPAN))


def cotangent(got, pick, out_t, lse, ids):
    width = got.shape[1]
    whole = pl.BlockSpec(memory_space=pltpu.VMEM)
    return pl.pallas_call(
        cotangent_kernel,
        in_specs=[whole] * 5,
        out_specs=[whole] * 3,
        out_shape=[
            jax.ShapeDtypeStruct((SPAN, width), bf16),
            jax.ShapeDtypeStruct((width, SPAN), bf16),
            jax.ShapeDtypeStruct((2 * HEADS + 8, SPAN), f32),
        ],
        compiler_params=params(),
        name="cotangent",
    )(got, pick, out_t, lse, ids)


def pick_other(stats, wanted):
    group = 4
    rows = 2 * HEADS

    def body(k, acc):
        spans = [stats[group * k + j] for j in range(group)]
        values = jnp.concatenate([span[:rows] for span in spans], axis=1)
        ids = jnp.concatenate([span[rows : rows + 1] for span in spans], axis=1)
        high = values.astype(bf16)
        rest = values - high.astype(f32)
        middle = rest.astype(bf16)
        low = (rest - middle.astype(f32)).astype(bf16)
        hits = jnp.where(wanted == ids, 1.0, 0.0).astype(bf16)
        return acc + mm(jnp.concatenate([high, middle, low], axis=0), hits, NT)

    acc = lax.fori_loop(0, stats.shape[0] // group, body, jnp.zeros((3 * rows, SPAN), f32))
    return acc[:rows] + (acc[rows : 2 * rows] + acc[2 * rows :])


def backward_kernel(
    scale, stats, wanted, mine, inverse, probs, k_own, k_prev, v_own, v_prev, g_own, g_t,
    grads, factor_s, delta_s, inner_s, weight_s, dscore_s, dq_s,
):
    step = pl.program_id(0)

    @pl.when(step == 0)
    def _():
        other = pick_other(stats, wanted[...])
        lse_a, d_a = mine[:HEADS, :], mine[HEADS : 2 * HEADS, :]
        lse_b, d_b = other[:HEADS], other[HEADS:]
        peak = jnp.maximum(lse_a, lse_b)
        total = peak + jnp.log(jnp.exp(lse_a - peak) + jnp.exp(lse_b - peak))
        share = jnp.exp(lse_a - total)
        factor_s[...] = share * inverse[...]
        delta_s[...] = share * d_a + jnp.exp(lse_b - total) * d_b

    half = PAIR // 2
    for p in range(BLOCK // PAIR):
        pair = (BLOCK // PAIR) * step + p
        lanes = lanes_of(pair)
        own = k_own[:, lanes]
        keys_t = jnp.concatenate([k_prev[:, lanes].T, own.T], axis=1)
        queries = head_masks((own.astype(f32) * scale).astype(bf16))
        cotangents = head_masks(g_own[:, lanes])
        for h in range(2):
            cotangent_t = half_rows(g_t[p * PAIR : (p + 1) * PAIR, :], h)
            inner_s[p, h, :SPAN] = mm(v_prev[:, lanes], cotangent_t)
            inner_s[p, h, SPAN:] = mm(v_own[:, lanes], cotangent_t)
        for h in range(2):
            factor = factor_s[pl.ds(2 * pair + h, 1), :]
            delta = delta_s[pl.ds(2 * pair + h, 1), :]
            queried = slice(h * SPAN, (h + 1) * SPAN)
            for part in chunks():
                weight = probs[2 * p + h, part].astype(f32) * factor
                weight_s[p, part, queried] = weight.astype(bf16)
                dscore_s[p, part, queried] = (weight * (inner_s[p, h, part] - delta)).astype(bf16)
        for h in range(2):
            part = slice(h * half, (h + 1) * half)
            dq_s[p, part, :] = mm(keys_t[part], dscore_s[p, :, h * SPAN : (h + 1) * SPAN])
        dv = mm(weight_s[p], jnp.concatenate(cotangents, axis=0))
        grads[1, :, lanes] = dv.astype(bf16)
        dk = mm(dscore_s[p], jnp.concatenate(queries, axis=0))
        grads[0, :SPAN, lanes] = dk[:SPAN].astype(bf16)
        grads[0, SPAN:, lanes] = (dk[SPAN:] + dq_s[p].T * scale).astype(bf16)


def backward(stats, wanted, mine, inverse, probs, k_own, k_prev, v_own, v_prev, g_own, g_t, scale):
    width = k_own.shape[1]
    square = pl.BlockSpec((HEADS * BLOCK // width, 2 * SPAN, SPAN), lambda i: (i, 0, 0))
    out = jax.ShapeDtypeStruct((2, 2 * SPAN, width), bf16)
    return pl.pallas_call(
        functools.partial(backward_kernel, scale),
        grid=(width // BLOCK,),
        in_specs=[whole_of(a) for a in (stats, wanted, mine, inverse)]
        + [square]
        + [whole_of(k_own)] * 5
        + [pl.BlockSpec((BLOCK, SPAN), lambda i: (i, 0))],
        out_specs=whole_of(out),
        out_shape=out,
        scratch_shapes=[
            pltpu.VMEM((HEADS, SPAN), f32),
            pltpu.VMEM((HEADS, SPAN), f32),
            pltpu.VMEM((BLOCK // PAIR, 2, 2 * SPAN, SPAN), f32),
            pltpu.VMEM((BLOCK // PAIR, 2 * SPAN, 2 * SPAN), bf16),
            pltpu.VMEM((BLOCK // PAIR, 2 * SPAN, 2 * SPAN), bf16),
            pltpu.VMEM((BLOCK // PAIR, PAIR, SPAN), f32),
        ],
        compiler_params=params(),
        name="backward",
    )(stats, wanted, mine, inverse, probs, k_own, k_prev, v_own, v_prev, g_own, g_t)


def small_params():
    return pltpu.CompilerParams(vmem_limit_bytes=VMEM_LIMIT // 4)


def cut_rows(total, low, leave, keep, cols):
    rows, width = total.shape
    cut = total.reshape(rows // (2 * low), 2, low, width)
    leave[:, cols] = cut[:, 1].reshape(rows // 2, width).astype(bf16)
    keep[:, cols] = cut[:, 0].reshape(rows // 2, width).astype(bf16)


def first_fold_kernel(edges, lows, x_t, grads, other_k, other_v, *outs):
    width = grads.shape[2]
    for part, low in enumerate(lows):
        for start in range(edges[part], edges[part + 1], BLOCK):
            kind, cols = start // width, slice(start % width, start % width + BLOCK)
            other = (other_k, other_v)[kind]
            total = mm(x_t[...], grads[kind, :, cols]) + other[:, cols].astype(f32)
            inside = slice(start - edges[part], start - edges[part] + BLOCK)
            cut_rows(total, low, outs[2 * part], outs[2 * part + 1], inside)


def fold_kernel(lows, *refs):
    outs = refs[2 * len(lows) :]
    for k, low in enumerate(lows):
        total = refs[2 * k][...].astype(f32) + refs[2 * k + 1][...].astype(f32)
        cut_rows(total, low, outs[2 * k], outs[2 * k + 1], slice(0, total.shape[1]))


def call_fold(kernel, operands, rows, widths, name):
    shapes = [jax.ShapeDtypeStruct((rows, w), bf16) for w in widths for _ in range(2)]
    whole = pl.BlockSpec(memory_space=pltpu.VMEM)
    outs = pl.pallas_call(
        kernel,
        in_specs=[whole] * len(operands),
        out_specs=[whole] * len(shapes),
        out_shape=shapes,
        compiler_params=small_params(),
        name=name,
    )(*operands)
    return [(outs[2 * k], outs[2 * k + 1]) for k in range(len(widths))]


def place_kernel(pick_t, y_own, y_next, sent):
    rows = y_own[...].astype(f32) + y_next[...].astype(f32)
    sent[...] = mm(pick_t[...], rows.astype(bf16)).astype(bf16)


def place_rows(pick_t, y_own, y_next):
    whole = pl.BlockSpec(memory_space=pltpu.VMEM)
    return pl.pallas_call(
        place_kernel,
        in_specs=[whole] * 3,
        out_specs=whole,
        out_shape=jax.ShapeDtypeStruct((pick_t.shape[0], y_own.shape[1]), bf16),
        compiler_params=small_params(),
        name="place_rows",
    )(pick_t, y_own, y_next)


def per_device(x2, out_grad, w_qk, w_v, sort_slot, source_pos):
    tdev, width = x2.shape
    part_rows = tdev // 2
    peers = lax.axis_size("ctx")
    near = peers // 2
    cap = 2 * tdev // peers
    slots = 2 * near * cap
    scale = (width // HEADS) ** (-0.5)
    chip = lax.axis_index("ctx")
    hround = lax.axis_index("round")
    side = chip // near
    both = ("ctx", "round")

    ring = span_ring(peers)
    span_of = [ring, [(peers - m) % peers for m in ring]]
    holder = [[spans.index(m) for m in range(peers)] for spans in span_of]

    def flat(c, r):
        return 2 * c + r

    every = [(c, r) for c in range(peers) for r in range(2)]
    onward = [
        (flat(holder[r][m], r), flat(holder[r][(m + 1) % peers], r))
        for m in range(peers)
        for r in range(2)
    ]
    backward_way = [(b, a) for a, b in onward]
    fetch = [(flat(span_of[r][c], r), flat(c, r)) for c, r in every]
    mirror = [(flat(c, r), flat((c + near) % peers, r)) for c, r in every]
    swap = [(flat(c, r), flat(c, 1 - r)) for c, r in every]
    swap_mirror = [(flat(c, r), flat((c + near) % peers, 1 - r)) for c, r in every]
    halves = [list(range(near)), list(range(near, peers))]

    def move(rows, route):
        return lax.ppermute(rows, both, route)

    def exchange(blocks):
        return lax.all_to_all(blocks, "ctx", 0, 0, axis_index_groups=halves, tiled=True)

    def my_part(rows):
        return lax.dynamic_slice_in_dim(rows, hround * part_rows, part_rows, 0)

    def their_part(rows):
        return lax.dynamic_slice_in_dim(rows, (1 - hround) * part_rows, part_rows, 0)

    own_spans = lax.dynamic_index_in_dim(sort_slot, hround, 0, keepdims=False) // SPAN
    spare = jnp.zeros((16, width - tdev), bf16)
    label = jnp.broadcast_to(own_spans.astype(bf16)[None, :], (16, tdev))
    label = jnp.concatenate([label, spare], axis=1)
    far_x = move(jnp.concatenate([my_part(x2), label], axis=0), mirror)
    far_x, half_g = lax.optimization_barrier((far_x, my_part(out_grad)))
    far_g = move(half_g, mirror)
    far_spans = far_x[part_rows, :tdev].astype(jnp.int32)
    far_x = far_x[:part_rows]

    def send_index(spans):
        tables = jnp.where(
            hround == 0, jnp.array(span_of[0], jnp.int32), jnp.array(span_of[1], jnp.int32)
        )
        held = spans[:, None] == tables[None, :]
        owner = jnp.sum(jnp.where(held, jnp.arange(peers, dtype=jnp.int32)[None, :], 0), axis=1)
        order = ordinal(owner, jnp.arange(tdev, dtype=jnp.int32))
        return jnp.where(owner // near == side, owner % near, peers) * 2 * cap + order

    near_index = send_index(own_spans)
    far_index = send_index(far_spans) + cap
    rolled = jnp.where(hround == 0, far_index, jnp.roll(far_index, part_rows, axis=0))
    send = one_hot(near_index, slots)
    send_far = one_hot(far_index, slots)
    send_far_rolled = one_hot(rolled, slots)
    sources = move(source_pos[0], fetch)
    group = sources // tdev
    is_near = group // near == side
    place = 2 * (group % near) * cap + jnp.where(is_near, 0, cap) + ordinal(group, sources)
    pick = one_hot(place, slots)

    def in_slots(rows, far_rows):
        far_rows = jnp.concatenate([far_rows, move(far_rows, swap)], axis=0)
        sent = mm(send, rows, TN) + mm(send_far_rolled, far_rows, TN)
        return sent.astype(bf16).reshape(near, 2 * cap, width)

    sent_x, sources = lax.optimization_barrier((in_slots(x2, far_x), sources))
    got_x = exchange(sent_x).reshape(slots, width)
    x_own = mm(pick, got_x).astype(bf16)
    x_prev = move(x_own, onward)
    far_g, _ = lax.optimization_barrier((far_g, x_own))
    k_own = mm(x_own, w_qk).astype(bf16)
    v_own = mm(x_own, w_v).astype(bf16)

    sent_g = in_slots(out_grad, far_g)
    x_prev, k_own, v_own, sent_g = lax.optimization_barrier((x_prev, k_own, v_own, sent_g))
    got_g = exchange(sent_g).reshape(slots, width)
    k_prev = mm(x_prev, w_qk).astype(bf16)
    v_prev = mm(x_prev, w_v).astype(bf16)
    lse, inverse, out_t, probs = forward(k_own, v_own, k_prev, v_prev, scale)
    ids = sources.astype(f32)
    g_own, g_t, mine = cotangent(got_g, pick, out_t, lse, ids[None, :])

    told = jnp.stack([move(mine, swap), move(mine, swap_mirror)])
    stats = exchange(jnp.broadcast_to(told[None], (near,) + told.shape))
    stats = stats.reshape((peers,) + mine.shape)

    each = width // (2 * peers)
    spot = jnp.arange(width // 2, dtype=jnp.int32)
    column = ((spot // each) ^ chip) * (2 * each) + spot % each
    x_both = jnp.concatenate([x_prev, x_own], axis=0)

    def columns_for(core):
        ordered = jnp.arange(width, dtype=jnp.int32)[None, :] == (column + core * each)[:, None]
        return mm(ordered.astype(bf16), x_both, NT).astype(bf16)

    x_ours, x_theirs = columns_for(hround), columns_for(1 - hround)
    stats, x_ours, x_theirs = lax.optimization_barrier((stats, x_ours, x_theirs))
    grads = backward(
        stats, ids[:, None], mine, inverse, probs, k_own, k_prev, v_own, v_prev, g_own, g_t, scale
    )

    y_prev = (mm(grads[0, :SPAN], w_qk, NT) + mm(grads[1, :SPAN], w_v, NT)).astype(bf16)
    y_next = move(y_prev, backward_way)

    x_theirs, _ = lax.optimization_barrier((x_theirs, y_prev))
    theirs = [move(mm(x_theirs, grads[k]).astype(bf16), swap) for k in range(2)]
    y_own = (mm(grads[0, SPAN:], w_qk, NT) + mm(grads[1, SPAN:], w_v, NT)).astype(bf16)

    bits = near.bit_length() - 1
    blocks = 2 * width // BLOCK
    edges = [BLOCK * ((blocks * k + 2) // 3) for k in range(4)]
    widths = [edges[k + 1] - edges[k] for k in range(3)]
    left = [list(range(bits + 1)) for _ in range(3)]
    pairs = None
    for turn in range(bits):
        turn_bits = [(k * bits // 3 + turn) % bits for k in range(3)]
        lows = [each << left[k].index(bit) for k, bit in enumerate(turn_bits)]
        if turn == 0:
            kernel = functools.partial(first_fold_kernel, edges, lows)
            operands = [x_ours, grads, theirs[0], theirs[1]]
        else:
            kernel = functools.partial(fold_kernel, lows)
            operands = [array for pair in pairs for array in pair]
        cuts = call_fold(kernel, operands, (width // 2) >> (turn + 1), widths, "fold")
        if turn == 0:
            y_next, cuts = lax.optimization_barrier((y_next, cuts))
            sent_y = place_rows(jnp.transpose(pick), y_own, y_next)
        pairs = []
        for k, (leave, keep) in enumerate(cuts):
            left[k].remove(turn_bits[k])
            route = [(flat(c, r), flat(c ^ (1 << turn_bits[k]), r)) for c, r in every]
            pairs.append((keep, move(leave, route)))
        if turn == 0:
            sent_y, pairs = lax.optimization_barrier((sent_y, pairs))
            got_y = exchange(sent_y.reshape(near, 2 * cap, width)).reshape(slots, width)
        if turn == 1:
            got_y, pairs = lax.optimization_barrier((got_y, pairs))
            rows_far = mm(send_far, got_y)
            rows_near = mm(send, got_y)
            from_core = jnp.concatenate([their_part(rows_far), their_part(rows_near)], axis=0)
            from_core = move(from_core.astype(bf16), swap)
            pairs, from_core = lax.optimization_barrier((pairs, from_core))
            from_core = from_core.astype(f32)
            crossing = move((my_part(rows_far) + from_core[:part_rows]).astype(bf16), mirror)
            grad_x = my_part(rows_near) + from_core[part_rows:] + crossing.astype(f32)
            grad_x = grad_x.astype(bf16)

    pairs, grad_x = lax.optimization_barrier((pairs, grad_x))
    summed = jnp.concatenate([a.astype(f32) + b.astype(f32) for a, b in pairs], axis=1)
    leaving = move(summed[each:].astype(bf16), mirror).astype(f32)
    weight_grads = (summed[:each] + leaving) * (tdev * peers) ** (-0.5)
    return (grad_x, weight_grads[:, :width], weight_grads[:, width:])


def solution(mesh):
    placed = (P("ctx", None), P("ctx", None), P(), P(), P(None, "ctx"), P("round", "ctx"))
    return jax.shard_map(
        per_device,
        mesh=mesh,
        in_specs=placed,
        out_specs=(P(("ctx", "round"), None), P(("ctx", "round"), None), P(("ctx", "round"), None)),
        check_vma=False,
    )
```

```python
import functools
import math

import jax
import jax.numpy as jnp
from jax import lax
from jax.experimental import pallas as pl
from jax.experimental.pallas import tpu as pltpu
from jax.sharding import PartitionSpec as P

HEADS = 16
SPAN = 256
LAYERS = 4
PAIR = 128
BLOCK = 256
VMEM_LIMIT = 56 * 2**20
CHUNK = 64

masked_score = -1000000000.0
NT = (((1,), (1,)), ((), ()))
TN = (((0,), (0,)), ((), ()))
f32 = jnp.float32
bf16 = jnp.bfloat16


def span_ring(peers):
    side = math.isqrt(peers // LAYERS)
    if side * side * LAYERS != peers or side % 2:
        return list(range(peers))
    columns = [(0, x) for x in range(side)]
    for y in range(1, side):
        xs = range(side - 1, 0, -1) if y % 2 else range(1, side)
        columns += [(y, x) for x in xs]
    columns += [(y, 0) for y in range(side - 1, 0, -1)]
    span_of = [0] * peers
    for k, (y, x) in enumerate(columns):
        for step in range(LAYERS):
            z = step if k % 2 == 0 else LAYERS - 1 - step
            span_of[(z * side + y) * side + x] = k * LAYERS + step
    return span_of


def ordinal(group, order):
    same = group[:, None] == group[None, :]
    before = order[None, :] < order[:, None]
    return jnp.sum((same & before).astype(jnp.int32), axis=1)


def one_hot(index, total):
    return (index[:, None] == jnp.arange(total, dtype=jnp.int32)[None, :]).astype(bf16)


def mm(a, b, dims=(((1,), (0,)), ((), ()))):
    return lax.dot_general(a, b, dims, preferred_element_type=f32)


def head_masks(block):
    lane = lax.broadcasted_iota(jnp.int32, block.shape, 1)
    zero = jnp.zeros_like(block)
    low = lane < PAIR // 2
    return jnp.where(low, block, zero), jnp.where(low, zero, block)


def half_rows(block_t, h):
    row = lax.broadcasted_iota(jnp.int32, block_t.shape, 0)
    return jnp.where((row < PAIR // 2) == (h == 0), block_t, jnp.zeros_like(block_t))


def chunks():
    return [slice(k, k + CHUNK) for k in range(0, 2 * SPAN, CHUNK)]


def lanes_of(pair):
    return pl.ds(pl.multiple_of(pair * PAIR, PAIR), PAIR)


def whole_of(array):
    zeros = (0,) * len(array.shape)
    return pl.BlockSpec(array.shape, lambda i: zeros)


def params():
    return pltpu.CompilerParams(vmem_limit_bytes=VMEM_LIMIT)


def forward_kernel(scale, k_own, v_own, k_prev, v_prev, lse, inverse, out_t, kept, scores):
    step = pl.program_id(0)
    half = PAIR // 2
    rows = lax.broadcasted_iota(jnp.int32, (SPAN, SPAN), 0)
    cols = lax.broadcasted_iota(jnp.int32, (SPAN, SPAN), 1)
    for p in range(BLOCK // PAIR):
        pair = (BLOCK // PAIR) * step + p
        lanes = lanes_of(pair)
        own = k_own[:, lanes]
        vals_t = jnp.concatenate([v_prev[:, lanes].T, v_own[:, lanes].T], axis=1)
        query_t = (own.T.astype(f32) * scale).astype(bf16)
        for h in range(2):
            mine = half_rows(query_t, h)
            scores[h, :SPAN] = mm(k_prev[:, lanes], mine)
            scores[h, SPAN:] = jnp.where(rows == cols, masked_score, mm(own, mine))
        for h in range(2):
            head = pl.ds(2 * pair + h, 1)
            top = jnp.max(scores[h], axis=0, keepdims=True)
            total = jnp.zeros((8, SPAN), f32)
            for part in chunks():
                probs = jnp.exp(scores[h, part] - top)
                total += jnp.sum(probs.reshape(CHUNK // 8, 8, SPAN), axis=0)
                kept[2 * p + h, part] = probs.astype(bf16)
            total = jnp.sum(total, axis=0, keepdims=True)
            lse[head, :] = top + jnp.log(total)
            inverse[head, :] = 1.0 / total
            first = p * PAIR + h * half
            out = mm(vals_t[h * half : (h + 1) * half], kept[2 * p + h])
            out_t[first : first + half, :] = out * (1.0 / total)


def forward(k_own, v_own, k_prev, v_prev, scale):
    width = k_own.shape[1]
    heads = HEADS * BLOCK // width
    rows = pl.BlockSpec((HEADS, SPAN), lambda i: (0, 0))
    return pl.pallas_call(
        functools.partial(forward_kernel, scale),
        grid=(width // BLOCK,),
        in_specs=[whole_of(k_own)] * 4,
        out_specs=[
            rows,
            rows,
            pl.BlockSpec((BLOCK, SPAN), lambda i: (i, 0)),
            pl.BlockSpec((heads, 2 * SPAN, SPAN), lambda i: (i, 0, 0)),
        ],
        out_shape=[
            jax.ShapeDtypeStruct((HEADS, SPAN), f32),
            jax.ShapeDtypeStruct((HEADS, SPAN), f32),
            jax.ShapeDtypeStruct((width, SPAN), f32),
            jax.ShapeDtypeStruct((HEADS, 2 * SPAN, SPAN), bf16),
        ],
        scratch_shapes=[pltpu.VMEM((2, 2 * SPAN, SPAN), f32)],
        compiler_params=params(),
        name="forward",
    )(k_own, v_own, k_prev, v_prev)


def cotangent_kernel(got, pick, out_t, lse, ids, g_out, g_t, stats):
    rows = mm(pick[...], got[...])
    g_out[...] = rows.astype(bf16)
    rows_t = rows.T
    g_t[...] = rows_t.astype(bf16)
    terms = (rows_t * out_t[...]).reshape(HEADS, PAIR // 2, SPAN)
    stats[:HEADS, :] = lse[...]
    stats[HEADS : 2 * HEADS, :] = jnp.sum(terms, axis=1)
    stats[2 * HEADS :, :] = jnp.broadcast_to(ids[...], (8, SPAN))


def cotangent(got, pick, out_t, lse, ids):
    width = got.shape[1]
    whole = pl.BlockSpec(memory_space=pltpu.VMEM)
    return pl.pallas_call(
        cotangent_kernel,
        in_specs=[whole] * 5,
        out_specs=[whole] * 3,
        out_shape=[
            jax.ShapeDtypeStruct((SPAN, width), bf16),
            jax.ShapeDtypeStruct((width, SPAN), bf16),
            jax.ShapeDtypeStruct((2 * HEADS + 8, SPAN), f32),
        ],
        compiler_params=params(),
        name="cotangent",
    )(got, pick, out_t, lse, ids)


def pick_other(stats, wanted):
    group = 4
    rows = 2 * HEADS

    def body(k, acc):
        spans = [stats[group * k + j] for j in range(group)]
        values = jnp.concatenate([span[:rows] for span in spans], axis=1)
        ids = jnp.concatenate([span[rows : rows + 1] for span in spans], axis=1)
        high = values.astype(bf16)
        rest = values - high.astype(f32)
        middle = rest.astype(bf16)
        low = (rest - middle.astype(f32)).astype(bf16)
        hits = jnp.where(wanted == ids, 1.0, 0.0).astype(bf16)
        return acc + mm(jnp.concatenate([high, middle, low], axis=0), hits, NT)

    acc = lax.fori_loop(0, stats.shape[0] // group, body, jnp.zeros((3 * rows, SPAN), f32))
    return acc[:rows] + (acc[rows : 2 * rows] + acc[2 * rows :])


def backward_kernel(
    scale, stats, wanted, mine, inverse, probs, k_own, k_prev, v_own, v_prev, g_own, g_t,
    grads, factor_s, delta_s, inner_s, weight_s, dscore_s, dq_s,
):
    step = pl.program_id(0)

    @pl.when(step == 0)
    def _():
        other = pick_other(stats, wanted[...])
        lse_a, d_a = mine[:HEADS, :], mine[HEADS : 2 * HEADS, :]
        lse_b, d_b = other[:HEADS], other[HEADS:]
        peak = jnp.maximum(lse_a, lse_b)
        total = peak + jnp.log(jnp.exp(lse_a - peak) + jnp.exp(lse_b - peak))
        share = jnp.exp(lse_a - total)
        factor_s[...] = share * inverse[...]
        delta_s[...] = share * d_a + jnp.exp(lse_b - total) * d_b

    half = PAIR // 2
    for p in range(BLOCK // PAIR):
        pair = (BLOCK // PAIR) * step + p
        lanes = lanes_of(pair)
        own = k_own[:, lanes]
        keys_t = jnp.concatenate([k_prev[:, lanes].T, own.T], axis=1)
        queries = head_masks((own.astype(f32) * scale).astype(bf16))
        cotangents = head_masks(g_own[:, lanes])
        for h in range(2):
            cotangent_t = half_rows(g_t[p * PAIR : (p + 1) * PAIR, :], h)
            inner_s[p, h, :SPAN] = mm(v_prev[:, lanes], cotangent_t)
            inner_s[p, h, SPAN:] = mm(v_own[:, lanes], cotangent_t)
        for h in range(2):
            factor = factor_s[pl.ds(2 * pair + h, 1), :]
            delta = delta_s[pl.ds(2 * pair + h, 1), :]
            queried = slice(h * SPAN, (h + 1) * SPAN)
            for part in chunks():
                weight = probs[2 * p + h, part].astype(f32) * factor
                weight_s[p, part, queried] = weight.astype(bf16)
                dscore_s[p, part, queried] = (weight * (inner_s[p, h, part] - delta)).astype(bf16)
        for h in range(2):
            part = slice(h * half, (h + 1) * half)
            dq_s[p, part, :] = mm(keys_t[part], dscore_s[p, :, h * SPAN : (h + 1) * SPAN])
        dv = mm(weight_s[p], jnp.concatenate(cotangents, axis=0))
        grads[1, :, lanes] = dv.astype(bf16)
        dk = mm(dscore_s[p], jnp.concatenate(queries, axis=0))
        grads[0, :SPAN, lanes] = dk[:SPAN].astype(bf16)
        grads[0, SPAN:, lanes] = (dk[SPAN:] + dq_s[p].T * scale).astype(bf16)


def backward(stats, wanted, mine, inverse, probs, k_own, k_prev, v_own, v_prev, g_own, g_t, scale):
    width = k_own.shape[1]
    square = pl.BlockSpec((HEADS * BLOCK // width, 2 * SPAN, SPAN), lambda i: (i, 0, 0))
    out = jax.ShapeDtypeStruct((2, 2 * SPAN, width), bf16)
    return pl.pallas_call(
        functools.partial(backward_kernel, scale),
        grid=(width // BLOCK,),
        in_specs=[whole_of(a) for a in (stats, wanted, mine, inverse)]
        + [square]
        + [whole_of(k_own)] * 5
        + [pl.BlockSpec((BLOCK, SPAN), lambda i: (i, 0))],
        out_specs=whole_of(out),
        out_shape=out,
        scratch_shapes=[
            pltpu.VMEM((HEADS, SPAN), f32),
            pltpu.VMEM((HEADS, SPAN), f32),
            pltpu.VMEM((BLOCK // PAIR, 2, 2 * SPAN, SPAN), f32),
            pltpu.VMEM((BLOCK // PAIR, 2 * SPAN, 2 * SPAN), bf16),
            pltpu.VMEM((BLOCK // PAIR, 2 * SPAN, 2 * SPAN), bf16),
            pltpu.VMEM((BLOCK // PAIR, PAIR, SPAN), f32),
        ],
        compiler_params=params(),
        name="backward",
    )(stats, wanted, mine, inverse, probs, k_own, k_prev, v_own, v_prev, g_own, g_t)


def small_params():
    return pltpu.CompilerParams(vmem_limit_bytes=VMEM_LIMIT // 4)


def cut_rows(total, low, leave, keep, cols):
    rows, width = total.shape
    cut = total.reshape(rows // (2 * low), 2, low, width)
    leave[:, cols] = cut[:, 1].reshape(rows // 2, width).astype(bf16)
    keep[:, cols] = cut[:, 0].reshape(rows // 2, width).astype(bf16)


def first_fold_kernel(edges, lows, x_t, grads, other_k, other_v, *outs):
    width = grads.shape[2]
    for part, low in enumerate(lows):
        for start in range(edges[part], edges[part + 1], BLOCK):
            kind, cols = start // width, slice(start % width, start % width + BLOCK)
            other = (other_k, other_v)[kind]
            total = mm(x_t[...], grads[kind, :, cols]) + other[:, cols].astype(f32)
            inside = slice(start - edges[part], start - edges[part] + BLOCK)
            cut_rows(total, low, outs[2 * part], outs[2 * part + 1], inside)


def fold_kernel(lows, *refs):
    outs = refs[2 * len(lows) :]
    for k, low in enumerate(lows):
        total = refs[2 * k][...].astype(f32) + refs[2 * k + 1][...].astype(f32)
        cut_rows(total, low, outs[2 * k], outs[2 * k + 1], slice(0, total.shape[1]))


def call_fold(kernel, operands, rows, widths, name):
    shapes = [jax.ShapeDtypeStruct((rows, w), bf16) for w in widths for _ in range(2)]
    whole = pl.BlockSpec(memory_space=pltpu.VMEM)
    outs = pl.pallas_call(
        kernel,
        in_specs=[whole] * len(operands),
        out_specs=[whole] * len(shapes),
        out_shape=shapes,
        compiler_params=small_params(),
        name=name,
    )(*operands)
    return [(outs[2 * k], outs[2 * k + 1]) for k in range(len(widths))]


def place_kernel(pick_t, y_own, y_next, sent):
    rows = y_own[...].astype(f32) + y_next[...].astype(f32)
    sent[...] = mm(pick_t[...], rows.astype(bf16)).astype(bf16)


def place_rows(pick_t, y_own, y_next):
    whole = pl.BlockSpec(memory_space=pltpu.VMEM)
    return pl.pallas_call(
        place_kernel,
        in_specs=[whole] * 3,
        out_specs=whole,
        out_shape=jax.ShapeDtypeStruct((pick_t.shape[0], y_own.shape[1]), bf16),
        compiler_params=small_params(),
        name="place_rows",
    )(pick_t, y_own, y_next)


def per_device(x2, out_grad, w_qk, w_v, sort_slot, source_pos):
    tdev, width = x2.shape
    part_rows = tdev // 2
    peers = lax.axis_size("ctx")
    near = peers // 2
    cap = 2 * tdev // peers
    slots = 2 * near * cap
    scale = (width // HEADS) ** (-0.5)
    chip = lax.axis_index("ctx")
    hround = lax.axis_index("round")
    side = chip // near
    both = ("ctx", "round")

    ring = span_ring(peers)
    span_of = [ring, [(peers - m) % peers for m in ring]]
    holder = [[spans.index(m) for m in range(peers)] for spans in span_of]

    def flat(c, r):
        return 2 * c + r

    every = [(c, r) for c in range(peers) for r in range(2)]
    onward = [
        (flat(holder[r][m], r), flat(holder[r][(m + 1) % peers], r))
        for m in range(peers)
        for r in range(2)
    ]
    backward_way = [(b, a) for a, b in onward]
    fetch = [(flat(span_of[r][c], r), flat(c, r)) for c, r in every]
    mirror = [(flat(c, r), flat((c + near) % peers, r)) for c, r in every]
    swap = [(flat(c, r), flat(c, 1 - r)) for c, r in every]
    swap_mirror = [(flat(c, r), flat((c + near) % peers, 1 - r)) for c, r in every]
    halves = [list(range(near)), list(range(near, peers))]

    def move(rows, route):
        return lax.ppermute(rows, both, route)

    def exchange(blocks):
        return lax.all_to_all(blocks, "ctx", 0, 0, axis_index_groups=halves, tiled=True)

    def my_part(rows):
        return lax.dynamic_slice_in_dim(rows, hround * part_rows, part_rows, 0)

    def their_part(rows):
        return lax.dynamic_slice_in_dim(rows, (1 - hround) * part_rows, part_rows, 0)

    own_spans = lax.dynamic_index_in_dim(sort_slot, hround, 0, keepdims=False) // SPAN
    spare = jnp.zeros((16, width - tdev), bf16)
    label = jnp.broadcast_to(own_spans.astype(bf16)[None, :], (16, tdev))
    label = jnp.concatenate([label, spare], axis=1)
    far_x = move(jnp.concatenate([my_part(x2), label], axis=0), mirror)
    far_x, half_g = lax.optimization_barrier((far_x, my_part(out_grad)))
    far_g = move(half_g, mirror)
    far_spans = far_x[part_rows, :tdev].astype(jnp.int32)
    far_x = far_x[:part_rows]

    def send_index(spans):
        tables = jnp.where(
            hround == 0, jnp.array(span_of[0], jnp.int32), jnp.array(span_of[1], jnp.int32)
        )
        held = spans[:, None] == tables[None, :]
        owner = jnp.sum(jnp.where(held, jnp.arange(peers, dtype=jnp.int32)[None, :], 0), axis=1)
        order = ordinal(owner, jnp.arange(tdev, dtype=jnp.int32))
        return jnp.where(owner // near == side, owner % near, peers) * 2 * cap + order

    near_index = send_index(own_spans)
    far_index = send_index(far_spans) + cap
    rolled = jnp.where(hround == 0, far_index, jnp.roll(far_index, part_rows, axis=0))
    send = one_hot(near_index, slots)
    send_far_rolled = one_hot(rolled, slots)
    sources = move(source_pos[0], fetch)
    group = sources // tdev
    is_near = group // near == side
    place = 2 * (group % near) * cap + jnp.where(is_near, 0, cap) + ordinal(group, sources)
    pick = one_hot(place, slots)

    def in_slots(rows, far_rows):
        far_rows = jnp.concatenate([far_rows, move(far_rows, swap)], axis=0)
        sent = mm(send, rows, TN) + mm(send_far_rolled, far_rows, TN)
        return sent.astype(bf16).reshape(near, 2 * cap, width)

    sent_x, sources = lax.optimization_barrier((in_slots(x2, far_x), sources))
    got_x = exchange(sent_x).reshape(slots, width)
    x_own = mm(pick, got_x).astype(bf16)
    x_prev = move(x_own, onward)
    far_g, _ = lax.optimization_barrier((far_g, x_own))
    k_own = mm(x_own, w_qk).astype(bf16)
    v_own = mm(x_own, w_v).astype(bf16)

    sent_g = in_slots(out_grad, far_g)
    x_prev, k_own, v_own, sent_g = lax.optimization_barrier((x_prev, k_own, v_own, sent_g))
    got_g = exchange(sent_g).reshape(slots, width)
    k_prev = mm(x_prev, w_qk).astype(bf16)
    v_prev = mm(x_prev, w_v).astype(bf16)
    lse, inverse, out_t, probs = forward(k_own, v_own, k_prev, v_prev, scale)
    ids = sources.astype(f32)
    g_own, g_t, mine = cotangent(got_g, pick, out_t, lse, ids[None, :])

    told = jnp.stack([move(mine, swap), move(mine, swap_mirror)])
    stats = exchange(jnp.broadcast_to(told[None], (near,) + told.shape))
    stats = stats.reshape((peers,) + mine.shape)

    each = width // (2 * peers)
    spot = jnp.arange(width // 2, dtype=jnp.int32)
    column = ((spot // each) ^ chip) * (2 * each) + spot % each
    x_both = jnp.concatenate([x_prev, x_own], axis=0)

    def columns_for(core):
        ordered = jnp.arange(width, dtype=jnp.int32)[None, :] == (column + core * each)[:, None]
        return mm(ordered.astype(bf16), x_both, NT).astype(bf16)

    x_ours, x_theirs = columns_for(hround), columns_for(1 - hround)
    stats, x_ours, x_theirs = lax.optimization_barrier((stats, x_ours, x_theirs))
    grads = backward(
        stats, ids[:, None], mine, inverse, probs, k_own, k_prev, v_own, v_prev, g_own, g_t, scale
    )

    y_prev = (mm(grads[0, :SPAN], w_qk, NT) + mm(grads[1, :SPAN], w_v, NT)).astype(bf16)
    y_next = move(y_prev, backward_way)

    mine_hot = one_hot(jnp.concatenate([my_part(far_index), my_part(near_index)]), slots)
    theirs_hot = one_hot(jnp.concatenate([their_part(far_index), their_part(near_index)]), slots)
    x_theirs, _ = lax.optimization_barrier((x_theirs, y_prev))
    theirs = [move(mm(x_theirs, grads[k]).astype(bf16), swap) for k in range(2)]
    y_own = (mm(grads[0, SPAN:], w_qk, NT) + mm(grads[1, SPAN:], w_v, NT)).astype(bf16)

    bits = near.bit_length() - 1
    blocks = 2 * width // BLOCK
    edges = [BLOCK * ((blocks * k + 2) // 3) for k in range(4)]
    widths = [edges[k + 1] - edges[k] for k in range(3)]
    left = [list(range(bits + 1)) for _ in range(3)]
    pairs = None
    for turn in range(bits):
        turn_bits = [(k * bits // 3 + turn) % bits for k in range(3)]
        lows = [each << left[k].index(bit) for k, bit in enumerate(turn_bits)]
        if turn == 0:
            kernel = functools.partial(first_fold_kernel, edges, lows)
            operands = [x_ours, grads, theirs[0], theirs[1]]
        else:
            kernel = functools.partial(fold_kernel, lows)
            operands = [array for pair in pairs for array in pair]
        cuts = call_fold(kernel, operands, (width // 2) >> (turn + 1), widths, "fold")
        if turn == 0:
            sent_y = place_rows(jnp.transpose(pick), y_own, y_next)
        pairs = []
        for k, (leave, keep) in enumerate(cuts):
            left[k].remove(turn_bits[k])
            route = [(flat(c, r), flat(c ^ (1 << turn_bits[k]), r)) for c, r in every]
            pairs.append((keep, move(leave, route)))
        if turn == 0:
            sent_y, pairs = lax.optimization_barrier((sent_y, pairs))
            got_y = exchange(sent_y.reshape(near, 2 * cap, width)).reshape(slots, width)
        if turn == 1:
            got_y, pairs = lax.optimization_barrier((got_y, pairs))
            from_core = move(mm(theirs_hot, got_y).astype(bf16), swap)
            my_rows = mm(mine_hot, got_y)
            pairs, from_core = lax.optimization_barrier((pairs, from_core))
            my_rows = my_rows + from_core.astype(f32)
            crossing = move(my_rows[:part_rows].astype(bf16), mirror)
            grad_x = (my_rows[part_rows:] + crossing.astype(f32)).astype(bf16)

    pairs, grad_x = lax.optimization_barrier((pairs, grad_x))
    summed = jnp.concatenate([a.astype(f32) + b.astype(f32) for a, b in pairs], axis=1)
    leaving = move(summed[each:].astype(bf16), mirror).astype(f32)
    weight_grads = (summed[:each] + leaving) * (tdev * peers) ** (-0.5)
    return (grad_x, weight_grads[:, :width], weight_grads[:, width:])


def solution(mesh):
    placed = (P("ctx", None), P("ctx", None), P(), P(), P(None, "ctx"), P("round", "ctx"))
    return jax.shard_map(
        per_device,
        mesh=mesh,
        in_specs=placed,
        out_specs=(P(("ctx", "round"), None), P(("ctx", "round"), None), P(("ctx", "round"), None)),
        check_vma=False,
    )
```

```python
import functools
import math

import jax
import jax.numpy as jnp
from jax import lax
from jax.experimental import pallas as pl
from jax.experimental.pallas import tpu as pltpu
from jax.sharding import PartitionSpec as P

HEADS = 16
SPAN = 256
LAYERS = 4
PAIR = 128
BLOCK = 256
VMEM_LIMIT = 56 * 2**20
CHUNK = 64

masked_score = -1000000000.0
NT = (((1,), (1,)), ((), ()))
TN = (((0,), (0,)), ((), ()))
f32 = jnp.float32
bf16 = jnp.bfloat16


def span_ring(peers):
    side = math.isqrt(peers // LAYERS)
    if side * side * LAYERS != peers or side % 2:
        return list(range(peers))
    columns = [(0, x) for x in range(side)]
    for y in range(1, side):
        xs = range(side - 1, 0, -1) if y % 2 else range(1, side)
        columns += [(y, x) for x in xs]
    columns += [(y, 0) for y in range(side - 1, 0, -1)]
    span_of = [0] * peers
    for k, (y, x) in enumerate(columns):
        for step in range(LAYERS):
            z = step if k % 2 == 0 else LAYERS - 1 - step
            span_of[(z * side + y) * side + x] = k * LAYERS + step
    return span_of


def ordinal(group, order):
    same = group[:, None] == group[None, :]
    before = order[None, :] < order[:, None]
    return jnp.sum((same & before).astype(jnp.int32), axis=1)


def one_hot(index, total):
    return (index[:, None] == jnp.arange(total, dtype=jnp.int32)[None, :]).astype(bf16)


def mm(a, b, dims=(((1,), (0,)), ((), ()))):
    return lax.dot_general(a, b, dims, preferred_element_type=f32)


def head_masks(block):
    lane = lax.broadcasted_iota(jnp.int32, block.shape, 1)
    zero = jnp.zeros_like(block)
    low = lane < PAIR // 2
    return jnp.where(low, block, zero), jnp.where(low, zero, block)


def half_rows(block_t, h):
    row = lax.broadcasted_iota(jnp.int32, block_t.shape, 0)
    return jnp.where((row < PAIR // 2) == (h == 0), block_t, jnp.zeros_like(block_t))


def chunks():
    return [slice(k, k + CHUNK) for k in range(0, 2 * SPAN, CHUNK)]


def lanes_of(pair):
    return pl.ds(pl.multiple_of(pair * PAIR, PAIR), PAIR)


def whole_of(array):
    zeros = (0,) * len(array.shape)
    return pl.BlockSpec(array.shape, lambda i: zeros)


def params():
    return pltpu.CompilerParams(vmem_limit_bytes=VMEM_LIMIT)


def forward_kernel(scale, k_own, v_own, k_prev, v_prev, lse, inverse, out_t, kept, scores):
    step = pl.program_id(0)
    half = PAIR // 2
    rows = lax.broadcasted_iota(jnp.int32, (SPAN, SPAN), 0)
    cols = lax.broadcasted_iota(jnp.int32, (SPAN, SPAN), 1)
    for p in range(BLOCK // PAIR):
        pair = (BLOCK // PAIR) * step + p
        lanes = lanes_of(pair)
        own = k_own[:, lanes]
        vals_t = jnp.concatenate([v_prev[:, lanes].T, v_own[:, lanes].T], axis=1)
        query_t = (own.T.astype(f32) * scale).astype(bf16)
        for h in range(2):
            mine = half_rows(query_t, h)
            scores[h, :SPAN] = mm(k_prev[:, lanes], mine)
            scores[h, SPAN:] = jnp.where(rows == cols, masked_score, mm(own, mine))
        for h in range(2):
            head = pl.ds(2 * pair + h, 1)
            top = jnp.max(scores[h], axis=0, keepdims=True)
            total = jnp.zeros((8, SPAN), f32)
            for part in chunks():
                probs = jnp.exp(scores[h, part] - top)
                total += jnp.sum(probs.reshape(CHUNK // 8, 8, SPAN), axis=0)
                kept[2 * p + h, part] = probs.astype(bf16)
            total = jnp.sum(total, axis=0, keepdims=True)
            lse[head, :] = top + jnp.log(total)
            inverse[head, :] = 1.0 / total
            first = p * PAIR + h * half
            out = mm(vals_t[h * half : (h + 1) * half], kept[2 * p + h])
            out_t[first : first + half, :] = out * (1.0 / total)


def forward(k_own, v_own, k_prev, v_prev, scale):
    width = k_own.shape[1]
    heads = HEADS * BLOCK // width
    rows = pl.BlockSpec((HEADS, SPAN), lambda i: (0, 0))
    return pl.pallas_call(
        functools.partial(forward_kernel, scale),
        grid=(width // BLOCK,),
        in_specs=[whole_of(k_own)] * 4,
        out_specs=[
            rows,
            rows,
            pl.BlockSpec((BLOCK, SPAN), lambda i: (i, 0)),
            pl.BlockSpec((heads, 2 * SPAN, SPAN), lambda i: (i, 0, 0)),
        ],
        out_shape=[
            jax.ShapeDtypeStruct((HEADS, SPAN), f32),
            jax.ShapeDtypeStruct((HEADS, SPAN), f32),
            jax.ShapeDtypeStruct((width, SPAN), f32),
            jax.ShapeDtypeStruct((HEADS, 2 * SPAN, SPAN), bf16),
        ],
        scratch_shapes=[pltpu.VMEM((2, 2 * SPAN, SPAN), f32)],
        compiler_params=params(),
        name="forward",
    )(k_own, v_own, k_prev, v_prev)


def cotangent_kernel(got, pick, out_t, lse, ids, g_out, g_t, stats):
    rows = mm(pick[...], got[...])
    g_out[...] = rows.astype(bf16)
    rows_t = rows.T
    g_t[...] = rows_t.astype(bf16)
    terms = (rows_t * out_t[...]).reshape(HEADS, PAIR // 2, SPAN)
    stats[:HEADS, :] = lse[...]
    stats[HEADS : 2 * HEADS, :] = jnp.sum(terms, axis=1)
    stats[2 * HEADS :, :] = jnp.broadcast_to(ids[...], (8, SPAN))


def cotangent(got, pick, out_t, lse, ids):
    width = got.shape[1]
    whole = pl.BlockSpec(memory_space=pltpu.VMEM)
    return pl.pallas_call(
        cotangent_kernel,
        in_specs=[whole] * 5,
        out_specs=[whole] * 3,
        out_shape=[
            jax.ShapeDtypeStruct((SPAN, width), bf16),
            jax.ShapeDtypeStruct((width, SPAN), bf16),
            jax.ShapeDtypeStruct((2 * HEADS + 8, SPAN), f32),
        ],
        compiler_params=params(),
        name="cotangent",
    )(got, pick, out_t, lse, ids)


def pick_other(stats, wanted):
    group = 4
    rows = 2 * HEADS

    def body(k, acc):
        spans = [stats[group * k + j] for j in range(group)]
        values = jnp.concatenate([span[:rows] for span in spans], axis=1)
        ids = jnp.concatenate([span[rows : rows + 1] for span in spans], axis=1)
        high = values.astype(bf16)
        rest = values - high.astype(f32)
        middle = rest.astype(bf16)
        low = (rest - middle.astype(f32)).astype(bf16)
        hits = jnp.where(wanted == ids, 1.0, 0.0).astype(bf16)
        return acc + mm(jnp.concatenate([high, middle, low], axis=0), hits, NT)

    acc = lax.fori_loop(0, stats.shape[0] // group, body, jnp.zeros((3 * rows, SPAN), f32))
    return acc[:rows] + (acc[rows : 2 * rows] + acc[2 * rows :])


def backward_kernel(
    scale, stats, wanted, mine, inverse, probs, k_own, k_prev, v_own, v_prev, g_own, g_t,
    grads, factor_s, delta_s, inner_s, weight_s, dscore_s, dq_s,
):
    step = pl.program_id(0)

    @pl.when(step == 0)
    def _():
        other = pick_other(stats, wanted[...])
        lse_a, d_a = mine[:HEADS, :], mine[HEADS : 2 * HEADS, :]
        lse_b, d_b = other[:HEADS], other[HEADS:]
        peak = jnp.maximum(lse_a, lse_b)
        total = peak + jnp.log(jnp.exp(lse_a - peak) + jnp.exp(lse_b - peak))
        share = jnp.exp(lse_a - total)
        factor_s[...] = share * inverse[...]
        delta_s[...] = share * d_a + jnp.exp(lse_b - total) * d_b

    half = PAIR // 2
    for p in range(BLOCK // PAIR):
        pair = (BLOCK // PAIR) * step + p
        lanes = lanes_of(pair)
        own = k_own[:, lanes]
        keys_t = jnp.concatenate([k_prev[:, lanes].T, own.T], axis=1)
        queries = head_masks((own.astype(f32) * scale).astype(bf16))
        cotangents = head_masks(g_own[:, lanes])
        for h in range(2):
            cotangent_t = half_rows(g_t[p * PAIR : (p + 1) * PAIR, :], h)
            inner_s[p, h, :SPAN] = mm(v_prev[:, lanes], cotangent_t)
            inner_s[p, h, SPAN:] = mm(v_own[:, lanes], cotangent_t)
        for h in range(2):
            factor = factor_s[pl.ds(2 * pair + h, 1), :]
            delta = delta_s[pl.ds(2 * pair + h, 1), :]
            queried = slice(h * SPAN, (h + 1) * SPAN)
            for part in chunks():
                weight = probs[2 * p + h, part].astype(f32) * factor
                weight_s[p, part, queried] = weight.astype(bf16)
                dscore_s[p, part, queried] = (weight * (inner_s[p, h, part] - delta)).astype(bf16)
        for h in range(2):
            part = slice(h * half, (h + 1) * half)
            dq_s[p, part, :] = mm(keys_t[part], dscore_s[p, :, h * SPAN : (h + 1) * SPAN])
        dv = mm(weight_s[p], jnp.concatenate(cotangents, axis=0))
        grads[1, :, lanes] = dv.astype(bf16)
        dk = mm(dscore_s[p], jnp.concatenate(queries, axis=0))
        grads[0, :SPAN, lanes] = dk[:SPAN].astype(bf16)
        grads[0, SPAN:, lanes] = (dk[SPAN:] + dq_s[p].T * scale).astype(bf16)


def backward(stats, wanted, mine, inverse, probs, k_own, k_prev, v_own, v_prev, g_own, g_t, scale):
    width = k_own.shape[1]
    square = pl.BlockSpec((HEADS * BLOCK // width, 2 * SPAN, SPAN), lambda i: (i, 0, 0))
    out = jax.ShapeDtypeStruct((2, 2 * SPAN, width), bf16)
    return pl.pallas_call(
        functools.partial(backward_kernel, scale),
        grid=(width // BLOCK,),
        in_specs=[whole_of(a) for a in (stats, wanted, mine, inverse)]
        + [square]
        + [whole_of(k_own)] * 5
        + [pl.BlockSpec((BLOCK, SPAN), lambda i: (i, 0))],
        out_specs=whole_of(out),
        out_shape=out,
        scratch_shapes=[
            pltpu.VMEM((HEADS, SPAN), f32),
            pltpu.VMEM((HEADS, SPAN), f32),
            pltpu.VMEM((BLOCK // PAIR, 2, 2 * SPAN, SPAN), f32),
            pltpu.VMEM((BLOCK // PAIR, 2 * SPAN, 2 * SPAN), bf16),
            pltpu.VMEM((BLOCK // PAIR, 2 * SPAN, 2 * SPAN), bf16),
            pltpu.VMEM((BLOCK // PAIR, PAIR, SPAN), f32),
        ],
        compiler_params=params(),
        name="backward",
    )(stats, wanted, mine, inverse, probs, k_own, k_prev, v_own, v_prev, g_own, g_t)


def small_params():
    return pltpu.CompilerParams(vmem_limit_bytes=VMEM_LIMIT // 4)


def cut_rows(total, low, leave, keep, cols):
    rows, width = total.shape
    cut = total.reshape(rows // (2 * low), 2, low, width)
    leave[:, cols] = cut[:, 1].reshape(rows // 2, width).astype(bf16)
    keep[:, cols] = cut[:, 0].reshape(rows // 2, width).astype(bf16)


def first_fold_kernel(edges, lows, x_t, grads, other_k, other_v, *outs):
    width = grads.shape[2]
    for part, low in enumerate(lows):
        for start in range(edges[part], edges[part + 1], BLOCK):
            kind, cols = start // width, slice(start % width, start % width + BLOCK)
            other = (other_k, other_v)[kind]
            total = mm(x_t[...], grads[kind, :, cols]) + other[:, cols].astype(f32)
            inside = slice(start - edges[part], start - edges[part] + BLOCK)
            cut_rows(total, low, outs[2 * part], outs[2 * part + 1], inside)


def fold_kernel(lows, *refs):
    outs = refs[2 * len(lows) :]
    for k, low in enumerate(lows):
        total = refs[2 * k][...].astype(f32) + refs[2 * k + 1][...].astype(f32)
        cut_rows(total, low, outs[2 * k], outs[2 * k + 1], slice(0, total.shape[1]))


def call_fold(kernel, operands, rows, widths, name):
    shapes = [jax.ShapeDtypeStruct((rows, w), bf16) for w in widths for _ in range(2)]
    whole = pl.BlockSpec(memory_space=pltpu.VMEM)
    outs = pl.pallas_call(
        kernel,
        in_specs=[whole] * len(operands),
        out_specs=[whole] * len(shapes),
        out_shape=shapes,
        compiler_params=small_params(),
        name=name,
    )(*operands)
    return [(outs[2 * k], outs[2 * k + 1]) for k in range(len(widths))]


def place_kernel(pick_t, y_own, y_next, sent):
    rows = y_own[...].astype(f32) + y_next[...].astype(f32)
    sent[...] = mm(pick_t[...], rows.astype(bf16)).astype(bf16)


def place_rows(pick_t, y_own, y_next):
    whole = pl.BlockSpec(memory_space=pltpu.VMEM)
    return pl.pallas_call(
        place_kernel,
        in_specs=[whole] * 3,
        out_specs=whole,
        out_shape=jax.ShapeDtypeStruct((pick_t.shape[0], y_own.shape[1]), bf16),
        compiler_params=small_params(),
        name="place_rows",
    )(pick_t, y_own, y_next)


def per_device(x2, out_grad, w_qk, w_v, sort_slot, source_pos):
    tdev, width = x2.shape
    part_rows = tdev // 2
    peers = lax.axis_size("ctx")
    near = peers // 2
    cap = 2 * tdev // peers
    slots = 2 * near * cap
    scale = (width // HEADS) ** (-0.5)
    chip = lax.axis_index("ctx")
    hround = lax.axis_index("round")
    side = chip // near
    both = ("ctx", "round")

    ring = span_ring(peers)
    span_of = [ring, [(peers - m) % peers for m in ring]]
    holder = [[spans.index(m) for m in range(peers)] for spans in span_of]

    def flat(c, r):
        return 2 * c + r

    every = [(c, r) for c in range(peers) for r in range(2)]
    onward = [
        (flat(holder[r][m], r), flat(holder[r][(m + 1) % peers], r))
        for m in range(peers)
        for r in range(2)
    ]
    backward_way = [(b, a) for a, b in onward]
    fetch = [(flat(span_of[r][c], r), flat(c, r)) for c, r in every]
    mirror = [(flat(c, r), flat((c + near) % peers, r)) for c, r in every]
    swap = [(flat(c, r), flat(c, 1 - r)) for c, r in every]
    swap_mirror = [(flat(c, r), flat((c + near) % peers, 1 - r)) for c, r in every]
    halves = [list(range(near)), list(range(near, peers))]

    def move(rows, route):
        return lax.ppermute(rows, both, route)

    def exchange(blocks):
        return lax.all_to_all(blocks, "ctx", 0, 0, axis_index_groups=halves, tiled=True)

    def my_part(rows):
        return lax.dynamic_slice_in_dim(rows, hround * part_rows, part_rows, 0)

    def their_part(rows):
        return lax.dynamic_slice_in_dim(rows, (1 - hround) * part_rows, part_rows, 0)

    own_spans = lax.dynamic_index_in_dim(sort_slot, hround, 0, keepdims=False) // SPAN
    spare = jnp.zeros((16, width - tdev), bf16)
    label = jnp.broadcast_to(own_spans.astype(bf16)[None, :], (16, tdev))
    label = jnp.concatenate([label, spare], axis=1)
    far_x = move(jnp.concatenate([my_part(x2), label], axis=0), mirror)
    far_x, half_g = lax.optimization_barrier((far_x, my_part(out_grad)))
    far_g = move(half_g, mirror)
    far_spans = far_x[part_rows, :tdev].astype(jnp.int32)
    far_x = far_x[:part_rows]

    def send_index(spans):
        tables = jnp.where(
            hround == 0, jnp.array(span_of[0], jnp.int32), jnp.array(span_of[1], jnp.int32)
        )
        held = spans[:, None] == tables[None, :]
        owner = jnp.sum(jnp.where(held, jnp.arange(peers, dtype=jnp.int32)[None, :], 0), axis=1)
        order = ordinal(owner, jnp.arange(tdev, dtype=jnp.int32))
        return jnp.where(owner // near == side, owner % near, peers) * 2 * cap + order

    near_index = send_index(own_spans)
    far_index = send_index(far_spans) + cap
    rolled = jnp.where(hround == 0, far_index, jnp.roll(far_index, part_rows, axis=0))
    send = one_hot(near_index, slots)
    send_far_rolled = one_hot(rolled, slots)
    sources = move(source_pos[0], fetch)
    group = sources // tdev
    is_near = group // near == side
    place = 2 * (group % near) * cap + jnp.where(is_near, 0, cap) + ordinal(group, sources)
    pick = one_hot(place, slots)

    def in_slots(rows, far_rows):
        far_rows = jnp.concatenate([far_rows, move(far_rows, swap)], axis=0)
        sent = mm(send, rows, TN) + mm(send_far_rolled, far_rows, TN)
        return sent.astype(bf16).reshape(near, 2 * cap, width)

    sent_x, sources = lax.optimization_barrier((in_slots(x2, far_x), sources))
    got_x = exchange(sent_x).reshape(slots, width)
    x_own = mm(pick, got_x).astype(bf16)
    x_prev = move(x_own, onward)
    far_g, _ = lax.optimization_barrier((far_g, x_own))
    k_own = mm(x_own, w_qk).astype(bf16)
    v_own = mm(x_own, w_v).astype(bf16)

    sent_g = in_slots(out_grad, far_g)
    x_prev, k_own, v_own, sent_g = lax.optimization_barrier((x_prev, k_own, v_own, sent_g))
    got_g = exchange(sent_g).reshape(slots, width)
    k_prev = mm(x_prev, w_qk).astype(bf16)
    v_prev = mm(x_prev, w_v).astype(bf16)
    lse, inverse, out_t, probs = forward(k_own, v_own, k_prev, v_prev, scale)
    ids = sources.astype(f32)
    g_own, g_t, mine = cotangent(got_g, pick, out_t, lse, ids[None, :])

    told = jnp.stack([move(mine, swap), move(mine, swap_mirror)])
    stats = exchange(jnp.broadcast_to(told[None], (near,) + told.shape))
    stats = stats.reshape((peers,) + mine.shape)

    each = width // (2 * peers)
    spot = jnp.arange(width // 2, dtype=jnp.int32)
    column = ((spot // each) ^ chip) * (2 * each) + spot % each
    x_both = jnp.concatenate([x_prev, x_own], axis=0)

    def columns_for(core):
        ordered = jnp.arange(width, dtype=jnp.int32)[None, :] == (column + core * each)[:, None]
        return mm(ordered.astype(bf16), x_both, NT).astype(bf16)

    x_ours, x_theirs = columns_for(hround), columns_for(1 - hround)
    stats, x_ours, x_theirs = lax.optimization_barrier((stats, x_ours, x_theirs))
    grads = backward(
        stats, ids[:, None], mine, inverse, probs, k_own, k_prev, v_own, v_prev, g_own, g_t, scale
    )

    y_prev = (mm(grads[0, :SPAN], w_qk, NT) + mm(grads[1, :SPAN], w_v, NT)).astype(bf16)
    y_next = move(y_prev, backward_way)

    mine_hot = one_hot(jnp.concatenate([my_part(far_index), my_part(near_index)]), slots)
    theirs_hot = one_hot(jnp.concatenate([their_part(far_index), their_part(near_index)]), slots)
    x_theirs, _ = lax.optimization_barrier((x_theirs, y_prev))
    theirs = [move(mm(x_theirs, grads[k]).astype(bf16), swap) for k in range(2)]
    y_own = (mm(grads[0, SPAN:], w_qk, NT) + mm(grads[1, SPAN:], w_v, NT)).astype(bf16)

    bits = peers.bit_length() - 1
    blocks = 2 * width // BLOCK
    edges = [BLOCK * ((blocks * k + 2) // 3) for k in range(4)]
    widths = [edges[k + 1] - edges[k] for k in range(3)]
    left = [list(range(bits)) for _ in range(3)]
    pairs = None
    for turn in range(bits):
        turn_bits = [(k * bits // 3 + turn) % bits for k in range(3)]
        lows = [each << left[k].index(bit) for k, bit in enumerate(turn_bits)]
        if turn == 0:
            kernel = functools.partial(first_fold_kernel, edges, lows)
            operands = [x_ours, grads, theirs[0], theirs[1]]
        else:
            kernel = functools.partial(fold_kernel, lows)
            operands = [array for pair in pairs for array in pair]
        cuts = call_fold(kernel, operands, (width // 2) >> (turn + 1), widths, "fold")
        if turn == 0:
            sent_y = place_rows(jnp.transpose(pick), y_own, y_next)
        pairs = []
        for k, (leave, keep) in enumerate(cuts):
            left[k].remove(turn_bits[k])
            route = [(flat(c, r), flat(c ^ (1 << turn_bits[k]), r)) for c, r in every]
            pairs.append((keep, move(leave, route)))
        if turn == 0:
            sent_y, pairs = lax.optimization_barrier((sent_y, pairs))
            got_y = exchange(sent_y.reshape(near, 2 * cap, width)).reshape(slots, width)
        if turn == 1:
            got_y, pairs = lax.optimization_barrier((got_y, pairs))
            from_core = move(mm(theirs_hot, got_y).astype(bf16), swap)
            my_rows = mm(mine_hot, got_y)
            pairs, from_core = lax.optimization_barrier((pairs, from_core))
            my_rows = my_rows + from_core.astype(f32)
            crossing = move(my_rows[:part_rows].astype(bf16), mirror)
            grad_x = (my_rows[part_rows:] + crossing.astype(f32)).astype(bf16)

    pairs, grad_x = lax.optimization_barrier((pairs, grad_x))
    weight_grads = jnp.concatenate([a.astype(f32) + b.astype(f32) for a, b in pairs], axis=1)
    weight_grads = weight_grads * (tdev * peers) ** (-0.5)
    return (grad_x, weight_grads[:, :width], weight_grads[:, width:])


def solution(mesh):
    placed = (P("ctx", None), P("ctx", None), P(), P(), P(None, "ctx"), P("round", "ctx"))
    return jax.shard_map(
        per_device,
        mesh=mesh,
        in_specs=placed,
        out_specs=(P(("ctx", "round"), None), P(("ctx", "round"), None), P(("ctx", "round"), None)),
        check_vma=False,
    )
```
